512 devices in a mesh: frame: 8 (over y), head: 32 (over x, z), rep: 2 (over core).
Axes of the slice: x: 4, y: 8, z: 8, core: 2. Of those that a mesh axis runs over, the one named last changes fastest.
Arguments:
- queries: bfloat16 [32768, 4096], P(('rep', 'frame', 'head')), parts along dimension 0, may hold values from -64 to 64
- key_rows: bfloat16 [32768, 4096], P(('rep', 'frame', 'head')), parts along dimension 0, may hold values from -64 to 64
- values: bfloat16 [32768, 4096], P(('rep', 'frame', 'head')), parts along dimension 0, may hold values from -6 to 6
- slot_frame: int32 [32], replicated, may hold values from 0 to 31, as said below
- radial_tiles: int32 [160, 3], replicated, may hold values from 0 to 512, as said below
Outputs:
- attended: bfloat16 [32768, 4096], P(('rep', 'frame', 'head')), parts along dimension 0
The draws below stay inside these ranges and needn't reach their ends.
There are 2 independent parts, one for each index of `rep`. The reference program is written for one: setup_inputs(seed, part) draws one part's arguments, and reference() takes and returns one part's arrays. A program takes and returns all parts, laid end to end along the dimension named above; an argument that names none is the same for every part. Nothing has to cross between parts.
Inputs may be any that keep to these rules, and one draw needn't show every extreme that they name: Slot s (rows s * 512 to (s + 1) * 512 - 1) holds latent frame slot_frame[s]; every frame is held once, and slot_frame[s] // 4 == s // 4. `radial_tiles`: each row is (query frame, key frame, half-width). Half-width 0 marks an empty row. Every frame has a row pairing it with itself with half-width 512 // 2 or more; no pair of frames has two nonempty rows; the frames of a nonempty row may lie anywhere in the sequence.
All inputs are finite; a program needn't handle non-finite values.
Results may differ from the reference program's by a relative error of at most 0.008.
Values may be sent and summed in bfloat16 or wider, within the bound.
A program may use at most 128 MiB of HBM per device.

```python
import math
import jax
import jax.numpy as jnp
from jax import lax

HEADS = 32
HEAD_DIM = 128
FRAME_PIX = 512
FR_DEV = 4
LEVELS = 2
FRAMES = 32
ROWS = 16384
TILES = 160


def draw_queries(key, part):
    key = jax.random.fold_in(key, 1)
    drawn = jax.random.normal(key, (ROWS, HEADS * HEAD_DIM), jnp.float32)
    result = drawn
    return jnp.clip(result, -64.0, 64.0).astype(jnp.bfloat16)


def draw_key_rows(key, part):
    key = jax.random.fold_in(key, 2)
    drawn = jax.random.normal(key, (ROWS, HEADS * HEAD_DIM), jnp.float32)
    result = drawn
    return jnp.clip(result, -64.0, 64.0).astype(jnp.bfloat16)


def draw_slot_frame(key, part):
    key = jax.random.fold_in(key, 4)
    slot_ids = jnp.arange(FRAMES, dtype=jnp.int32)
    noise = jax.random.randint(key, (FRAMES,), 0, 1000)
    scores = slot_ids // FR_DEV * (1001 * FRAMES) + noise * FRAMES + slot_ids
    return jnp.argsort(scores, stable=True).astype(jnp.int32)


def draw_radial_tiles(key, part):
    key = jax.random.fold_in(key, 3)
    own_key, far_key = jax.random.split(key)
    query_ids = jnp.arange(FRAMES, dtype=jnp.int32)
    own_width = jax.random.randint(own_key, (FRAMES,), FRAME_PIX // 2, FRAME_PIX + 1)
    own_width = own_width.at[0].set(FRAME_PIX)
    columns = [jnp.stack([query_ids, query_ids, own_width], axis=1)]
    for level in range(1, LEVELS + 1):
        low_dist = 1 if level == 1 else FRAMES * 2 ** (level - 1) // 2 ** LEVELS
        high_dist = FRAMES * 2 ** level // 2 ** LEVELS
        for sign_index in range(2):
            sign = 1 - 2 * sign_index
            level_key = jax.random.fold_in(far_key, level * 2 + sign_index)
            dist_key, width_key = jax.random.split(level_key)
            distance = jax.random.randint(dist_key, (FRAMES,), low_dist, high_dist)
            width = jax.random.randint(width_key, (FRAMES,), FRAME_PIX // 2 ** (level + 1), FRAME_PIX // 2 ** level + 1)
            target = query_ids + sign * distance
            inside = (target >= 0) & (target < FRAMES)
            columns.append(jnp.stack([query_ids, jnp.where(inside, target, query_ids), jnp.where(inside, width, 0)], axis=1))
    return jnp.stack(columns, axis=1).reshape(TILES, 3).astype(jnp.int32)


def block_levels(key, shape, shards, low, top_value):
    gain, own = 1.0, jax.random.fold_in(key, 6)
    for position, parts in shards:
        draws = jnp.exp(jax.random.uniform(jax.random.fold_in(own, position), (parts,), jnp.float32, low / len(shards), top_value / len(shards)))
        gain = gain * jnp.repeat(draws, shape[position] // parts).reshape([-1 if axis == position else 1 for axis in range(len(shape))])
    return gain


def bell_draw(rng, shape, scale, bound, cuts=(), kind=jnp.bfloat16):
    factor_of = block_levels(rng, shape, cuts, -0.22, 0.18) if cuts else 1.0
    values = jax.random.normal(rng, shape, jnp.float32) * scale * factor_of
    return jnp.minimum(jnp.maximum(values, -bound), bound).astype(kind)


def setup_inputs(seed: int = 0, part: int = 0) -> dict:
    key_of = jax.random.split(jax.random.key(seed), 6)
    own_keys = jax.random.split(jax.random.fold_in(key_of[5], part), 6)
    return {
        "queries": draw_queries(jax.random.fold_in(jax.random.fold_in(key_of[5], part), 71), part),
        "key_rows": draw_key_rows(jax.random.fold_in(jax.random.fold_in(key_of[5], part), 71), part),
        "values": bell_draw(own_keys[2], (ROWS, HEADS * HEAD_DIM), 1.0, 6.0, ((0, 256),)),
        "slot_frame": draw_slot_frame(jax.random.fold_in(key_of[5], 71), part),
        "radial_tiles": draw_radial_tiles(jax.random.fold_in(key_of[5], 71), part),
    }


def update(carry_state, query_frame, keys_block, vals_block, key_pos, row_width, score_scale):
    row_top, row_total, weighted = carry_state
    positions = jnp.arange(query_frame.shape[0], dtype=jnp.int32)
    scores = jnp.einsum('phe,khe->phk', query_frame.astype(jnp.float32), keys_block.astype(jnp.float32)) * score_scale
    allowed = (jnp.abs(positions[:, None] - key_pos[None, :]) < row_width[None, :])[:, None, :]
    masked = jnp.where(allowed, scores, -1e+30)
    new_top = jnp.maximum(row_top, lax.optimization_barrier(jnp.max(masked, axis=-1)))
    weight = jnp.where(allowed, jnp.exp(masked - new_top[..., None]), 0.0)
    shrink = jnp.exp(row_top - new_top)
    row_total = row_total * shrink + lax.optimization_barrier(jnp.sum(weight, axis=-1))
    rounded = weight.astype(jnp.bfloat16).astype(jnp.float32)
    weighted = weighted * shrink[..., None] + jnp.einsum('phk,khe->phe', rounded, vals_block.astype(jnp.float32))
    return (new_top, row_total, weighted)

def reference(queries, key_rows, values, slot_frame, radial_tiles):
    score_scale = 1.0 / math.sqrt(HEAD_DIM)
    table = jnp.zeros((FRAMES, FRAMES), jnp.int32).at[radial_tiles[:, 0], radial_tiles[:, 1]].add(radial_tiles[:, 2])
    slot_width = table[slot_frame][:, slot_frame]
    shape_four = (FRAMES, FRAME_PIX, HEADS, HEAD_DIM)
    query_frames = queries.reshape(shape_four)
    key_frames = key_rows.reshape(shape_four)
    value_frames = values.reshape(shape_four)
    key_pos = jnp.arange(FRAME_PIX, dtype=jnp.int32)

    def one_slot(inputs):
        query_frame, widths = inputs
        start = (jnp.full((FRAME_PIX, HEADS), -1e+30, jnp.float32), jnp.zeros((FRAME_PIX, HEADS), jnp.float32), jnp.zeros((FRAME_PIX, HEADS, HEAD_DIM), jnp.float32))

        def visit(carry_state, item):
            keys_frame, vals_frame, tile_width = item
            row_width = jnp.full((FRAME_PIX,), tile_width, jnp.int32)

            def attend(carried):
                return update(carried, query_frame, keys_frame, vals_frame, key_pos, row_width, score_scale)

            def keep(carried):
                return carried
            return (lax.cond(tile_width > 0, attend, keep, carry_state), None)
        final, unused = lax.scan(visit, start, (key_frames, value_frames, widths))
        return (final[2] / final[1][..., None]).astype(jnp.bfloat16)
    output = lax.map(one_slot, (query_frames, slot_width))
    return output.reshape(FRAMES * FRAME_PIX, HEADS * HEAD_DIM)
```

```python
import functools
import math

import jax
import jax.numpy as jnp
from jax import lax
from jax.experimental import pallas as pl
from jax.experimental.pallas import tpu as pltpu
from jax.sharding import PartitionSpec as P

HEADS = 32
HEAD_DIM = 128
FRAME_PIX = 512
GROUPS = 8
GROUP_FRAMES = 4
CHUNK = 64
SLOTS = 32
ROOMS = (12, 13, 14, 32)
MESH = pl.DeviceIdType.MESH
SCALE = math.log2(math.e) / math.sqrt(HEAD_DIM)


def place():
    y = lax.axis_index("frame")
    xz = lax.axis_index("head")
    x = lax.div(xz, 8)
    z = lax.rem(xz, 8)
    return y, x, lax.div(z, 2), lax.rem(z, 2), lax.axis_index("rep")


def partner(t, y, zh):
    return lax.rem(y + 3 * t, 8), lax.rem(zh + t + lax.div(t, 8), 4)


def send(src, dst, send_sem, recv_sem, here, there):
    same = (here[0] == there[0]) & (here[1] == there[1])

    @pl.when(same)
    def _():
        pltpu.make_async_copy(src, dst, recv_sem).start()

    @pl.when(jnp.logical_not(same))
    def _():
        pltpu.make_async_remote_copy(
            src_ref=src,
            dst_ref=dst,
            send_sem=send_sem,
            recv_sem=recv_sem,
            device_id=there,
            device_id_type=MESH,
        ).start()


def greet(there):
    pl.semaphore_signal(
        pltpu.get_barrier_semaphore(), inc=1, device_id=there, device_id_type=MESH
    )


def wait_bytes(ref, sem):
    pltpu.make_async_copy(ref, ref, sem).wait()


def chunk_of(y, x, zh, zl):
    turn = lax.rem(x + 16 - y - zh, 4)
    return lax.rem(2 * zh + jnp.where(zl == 1, turn + 1, 8 - turn), 8)


def gather_kernel(
    capacity,
    lists_ref,
    q_ref,
    k_ref,
    v_ref,
    q_out,
    k_out,
    v_out,
    k_spread,
    v_spread,
    k_other,
    v_other,
    k_stage,
    v_stage,
    k_relay,
    v_relay,
    send_sem,
    recv_sem,
    relay_sem,
    quarter_sem,
):
    y, x, zh, zl, core = place()
    z = 2 * zh + zl
    here = (y, x * 8 + z, core)
    right, left = lax.rem(x + 1, 4), lax.rem(x + 3, 4)

    def at(x2, zl2):
        return (y, x2 * 8 + 2 * zh + zl2, core)

    chunk = chunk_of(y, x, zh, zl)
    same_chunk = chunk == z
    same_query = lax.rem(y, 2) == zl

    def greet_senders(t, carry):
        y1, x1 = lax.rem(t, 8), lax.div(t, 8)

        @pl.when((y1 != y) | (x1 != x) | (chunk != z))
        def _():
            greet((y1, x1 * 8 + chunk, core))

        y2, z2 = 2 * lax.rem(t, 4) + zl, lax.div(t, 4)

        @pl.when((y2 != y) | (z2 != z))
        def _():
            greet((y2, x * 8 + z2, core))

        return carry

    lax.fori_loop(0, HEADS, greet_senders, 0)
    for mate in (at(right, zl), at(left, zl), at(x, 1 - zl)):
        greet(mate)
    pl.semaphore_wait(
        pltpu.get_barrier_semaphore(),
        2 * HEADS + 3 - same_chunk.astype(jnp.int32) - same_query.astype(jnp.int32),
    )

    def spread(source, landing, number):
        def step(t, carry):
            y2, zh2 = partner(t, y, zh)
            off = lax.rem(z - 2 * zh2 + 11, 8) - 3
            zl2 = (off > 0).astype(jnp.int32)
            turn = jnp.where(off > 0, off - 1, -off)
            x2 = lax.rem(turn + y2 + zh2, 4)
            head = y2 * 4 + zh2
            send(
                source.at[:, pl.ds(pl.multiple_of(head * HEAD_DIM, HEAD_DIM), HEAD_DIM)],
                landing.at[lax.div(t, 4), x],
                send_sem.at[number],
                quarter_sem.at[4 * number + lax.div(t, 8)],
                here,
                (y2, x2 * 8 + 2 * zh2 + zl2, core),
            )
            return carry

        lax.fori_loop(0, HEADS, step, 0)

    def send_queries():
        def step(t, carry):
            y2, zh2 = partner(t, y, zh)
            z2 = 2 * zh2 + lax.rem(y, 2)
            head = y2 * 4 + zh2
            send(
                q_ref.at[:, pl.ds(pl.multiple_of(head * HEAD_DIM, HEAD_DIM), HEAD_DIM)],
                q_out.at[lax.div(y, 2), z],
                send_sem.at[2],
                recv_sem.at[2],
                here,
                (y2, x * 8 + z2, core),
            )
            return carry

        lax.fori_loop(0, HEADS, step, 0)

    def remote(src, dst, sent, received, there):
        return pltpu.make_async_remote_copy(
            src_ref=src,
            dst_ref=dst,
            send_sem=sent,
            recv_sem=received,
            device_id=there,
            device_id_type=MESH,
        )

    def swap(spread_ref, other_ref, number):
        for quarter in range(4):
            part = pl.ds(2 * quarter, 2)
            wait_bytes(spread_ref.at[part], quarter_sem.at[4 * number + quarter])
            remote(
                spread_ref.at[part],
                other_ref.at[part],
                send_sem.at[3 + number],
                recv_sem.at[3 + number],
                at(x, 1 - zl),
            ).start()

    def spot(slot, side):
        source = lax.div(chunk_of(y, x, zh, zl if side == 0 else 1 - zl), 2)
        eighth = lax.rem(3 * (y + 8 - lax.div(slot, GROUP_FRAMES)), 8)
        quarter = lax.rem(zh + 12 - source - eighth, 4)
        return 2 * quarter + lax.div(eighth, 4), lax.rem(slot, GROUP_FRAMES)

    mates = (right, left, lax.rem(x + 2, 4), x)

    def to_mates(side, spread_ref, stage, relay, landing, number):
        def pick(p, carry):
            for mate, x2 in enumerate(mates):
                slot = lists_ref[(2 * x2 + zl) * SLOTS + p]
                stage[side, mate, p] = spread_ref[spot(slot, side)]
            return carry

        lax.fori_loop(0, capacity, pick, 0)
        rows = landing.at[:, chunk_of(y, x, zh, zl if side == 0 else 1 - zl)]
        sent, landed = send_sem.at[5 + number], recv_sem.at[5 + number]
        by = right if side == 0 else left
        passed = relay_sem.at[2 * number + side]
        remote(stage.at[side, 2], relay.at[side], sent, passed, at(by, zl)).start()
        remote(stage.at[side, 0], rows, sent, landed, at(right, zl)).start()
        remote(stage.at[side, 1], rows, sent, landed, at(left, zl)).start()
        pltpu.make_async_copy(stage.at[side, 3], rows, landed).start()

    def pass_on(side, relay, landing, number):
        wait_bytes(relay.at[side], relay_sem.at[2 * number + side])
        owner, there = (left, right) if side == 0 else (right, left)
        rows = landing.at[:, chunk_of(y, owner, zh, zl if side == 0 else 1 - zl)]
        remote(
            relay.at[side], rows, send_sem.at[7 + number], recv_sem.at[5 + number], at(there, zl)
        ).start()

    spread(k_ref, k_spread, 0)
    spread(v_ref, v_spread, 1)
    swap(k_spread, k_other, 0)
    to_mates(0, k_spread, k_stage, k_relay, k_out, 0)
    send_queries()
    swap(v_spread, v_other, 1)
    to_mates(0, v_spread, v_stage, v_relay, v_out, 1)
    wait_bytes(k_other, recv_sem.at[3])
    to_mates(1, k_other, k_stage, k_relay, k_out, 0)
    pass_on(0, k_relay, k_out, 0)
    wait_bytes(v_other, recv_sem.at[4])
    to_mates(1, v_other, v_stage, v_relay, v_out, 1)
    pass_on(0, v_relay, v_out, 1)
    pass_on(1, k_relay, k_out, 0)
    pass_on(1, v_relay, v_out, 1)
    wait_bytes(k_spread, send_sem.at[3])
    wait_bytes(v_spread, send_sem.at[4])

    def wait_sent(number, own_copy):
        @pl.when(own_copy)
        def _():
            wait_bytes(k_ref.at[:, pl.ds(0, (HEADS - 1) * HEAD_DIM)], send_sem.at[number])

        @pl.when(jnp.logical_not(own_copy))
        def _():
            wait_bytes(k_spread, send_sem.at[number])

    own_copy = same_chunk & (lax.rem(y + zh, 4) == x)
    wait_sent(0, own_copy)
    wait_sent(1, own_copy)
    wait_sent(2, same_query)
    for number, stage, relay in ((0, k_stage, k_relay), (1, v_stage, v_relay)):
        wait_bytes(stage.at[:, pl.ds(0, 3)], send_sem.at[5 + number])
        wait_bytes(relay, send_sem.at[7 + number])
    wait_bytes(q_out, recv_sem.at[2])
    wait_bytes(k_out, recv_sem.at[5])
    wait_bytes(v_out, recv_sem.at[6])


def gather(capacity, lists, queries, key_rows, values):
    any_space = pl.BlockSpec(memory_space=pl.ANY)
    pieces = (GROUP_FRAMES, GROUPS, CHUNK, HEAD_DIM)
    picked = (capacity, GROUPS, CHUNK, HEAD_DIM)
    scratch = [(GROUPS, GROUP_FRAMES)] * 4 + [(2, 4, capacity)] * 2 + [(2, capacity)] * 2
    return pl.pallas_call(
        functools.partial(gather_kernel, capacity),
        out_shape=[jax.ShapeDtypeStruct(shape, jnp.bfloat16) for shape in (pieces, picked, picked)],
        in_specs=[pl.BlockSpec(memory_space=pltpu.SMEM), any_space, any_space, any_space],
        out_specs=[any_space] * 3,
        scratch_shapes=[
            *(pltpu.VMEM((*shape, CHUNK, HEAD_DIM), jnp.bfloat16) for shape in scratch),
            pltpu.SemaphoreType.DMA((9,)),
            pltpu.SemaphoreType.DMA((7,)),
            pltpu.SemaphoreType.DMA((4,)),
            pltpu.SemaphoreType.DMA((8,)),
        ],
        compiler_params=pltpu.CompilerParams(
            collective_id=ROOMS.index(capacity), has_side_effects=True, vmem_limit_bytes=40 * 2**20
        ),
    )(lists, queries, key_rows, values)


BLOCK = 256


def attend_kernel(info_ref, q_ref, k_ref, v_ref, o_ref, apart, ones, top, weighted):
    square = (FRAME_PIX, FRAME_PIX)
    apart[...] = jnp.abs(
        lax.broadcasted_iota(jnp.int32, square, 0) - lax.broadcasted_iota(jnp.int32, square, 1)
    )
    ones[...] = jnp.ones_like(ones)

    def tile(own, position, width, first, narrow):
        for block in range(FRAME_PIX // BLOCK):
            rows = pl.ds(block * BLOCK, BLOCK)
            near = pl.ds(block * 128, 384) if narrow else pl.ds(0, FRAME_PIX)
            scores = lax.dot_general(
                q_ref[own, rows, :],
                k_ref[position, near, :],
                (((1,), (1,)), ((), ())),
                preferred_element_type=jnp.float32,
            )
            masked = jnp.where(apart[rows, near] < width, scores * SCALE, -1e30)
            high = jnp.max(masked, axis=1, keepdims=True)
            if first:
                new_top = high
            else:
                old_top = top[rows, :]
                new_top = jnp.maximum(old_top, high)
            weight = jnp.exp2(masked - new_top)
            product = jnp.dot(
                weight.astype(jnp.bfloat16),
                jnp.concatenate([v_ref[position, near, :], ones[near, :]], axis=1),
                preferred_element_type=jnp.float32,
            )
            if first:
                weighted[rows, :] = product
            else:
                weighted[rows, :] = weighted[rows, :] * jnp.exp2(old_top - new_top) + product
            top[rows, :] = new_top

    def one_frame(own, carry):
        code = info_ref[own * SLOTS]
        tile(own, lax.shift_right_logical(code, 10), lax.bitwise_and(code, 1023), True, False)

        def visit(number, inner):
            code = info_ref[own * SLOTS + number]
            position, width = lax.shift_right_logical(code, 10), lax.bitwise_and(code, 1023)

            @pl.when(width > 128)
            def _():
                tile(own, position, width, False, False)

            @pl.when(width <= 128)
            def _():
                tile(own, position, width, False, True)

            return inner

        lax.fori_loop(1, info_ref[GROUP_FRAMES * SLOTS + own], visit, 0)
        o_ref[own] = (weighted[:, :HEAD_DIM] / weighted[:, HEAD_DIM:]).astype(jnp.bfloat16)
        return carry

    lax.fori_loop(0, GROUP_FRAMES, one_frame, 0)


def attend(info, q_local, keys, vals):
    capacity = keys.shape[0]
    vmem = pl.BlockSpec(memory_space=pltpu.VMEM)
    outcome = pl.pallas_call(
        attend_kernel,
        out_shape=jax.ShapeDtypeStruct((GROUP_FRAMES, FRAME_PIX, HEAD_DIM), jnp.bfloat16),
        in_specs=[pl.BlockSpec(memory_space=pltpu.SMEM), vmem, vmem, vmem],
        out_specs=vmem,
        scratch_shapes=[
            pltpu.VMEM((FRAME_PIX, FRAME_PIX), jnp.int32),
            pltpu.VMEM((FRAME_PIX, HEAD_DIM), jnp.bfloat16),
            pltpu.VMEM((FRAME_PIX, 1), jnp.float32),
            pltpu.VMEM((FRAME_PIX, 2 * HEAD_DIM), jnp.float32),
        ],
        compiler_params=pltpu.CompilerParams(vmem_limit_bytes=40 * 2**20),
    )(
        info,
        q_local.reshape(GROUP_FRAMES, FRAME_PIX, HEAD_DIM),
        keys.reshape(capacity, FRAME_PIX, HEAD_DIM),
        vals.reshape(capacity, FRAME_PIX, HEAD_DIM),
    )
    return outcome.reshape(GROUP_FRAMES, GROUPS, CHUNK, HEAD_DIM)


def return_kernel(o_ref, out_ref, send_sem, recv_sem):
    y, x, zh, zl, core = place()
    z = 2 * zh + zl
    here = (y, x * 8 + z, core)
    head = y * 4 + zh
    same = lax.rem(y, 2) == zl

    def greet_senders(t, carry):
        y2, z2 = lax.rem(t, 8), 2 * lax.div(t, 8) + lax.rem(y, 2)

        @pl.when((y2 != y) | (z2 != z))
        def _():
            greet((y2, x * 8 + z2, core))

        return carry

    lax.fori_loop(0, HEADS, greet_senders, 0)
    pl.semaphore_wait(pltpu.get_barrier_semaphore(), HEADS - same.astype(jnp.int32))

    def step(t, carry):
        number = lax.rem(lax.div(y, 2) + t + lax.div(t, 8), 4)
        y2 = 2 * number + zl
        z2 = lax.rem(z + 3 * t, 8)
        send(
            o_ref.at[number, z2],
            out_ref.at[head],
            send_sem,
            recv_sem,
            here,
            (y2, x * 8 + z2, core),
        )
        return carry

    lax.fori_loop(0, HEADS, step, 0)
    sent = out_ref.at[pl.ds(0, HEADS - 1)]

    @pl.when(same)
    def _():
        wait_bytes(sent, send_sem)

    @pl.when(jnp.logical_not(same))
    def _():
        wait_bytes(out_ref, send_sem)

    wait_bytes(out_ref, recv_sem)


def send_back(outcome):
    any_space = pl.BlockSpec(memory_space=pl.ANY)
    by_head = pl.pallas_call(
        return_kernel,
        out_shape=jax.ShapeDtypeStruct((HEADS, CHUNK, HEAD_DIM), jnp.bfloat16),
        in_specs=[any_space],
        out_specs=any_space,
        scratch_shapes=[pltpu.SemaphoreType.DMA, pltpu.SemaphoreType.DMA],
        compiler_params=pltpu.CompilerParams(collective_id=len(ROOMS), has_side_effects=True),
    )(outcome)
    return by_head.transpose(1, 0, 2).reshape(CHUNK, HEADS * HEAD_DIM)


def on_device(queries, key_rows, values, slot_frame, radial_tiles):
    on_query = slot_frame[:, None] == radial_tiles[None, :, 0]
    on_key = slot_frame[:, None] == radial_tiles[None, :, 1]
    slot_width = jnp.dot(
        on_query.astype(jnp.int32) * radial_tiles[None, :, 2], on_key.astype(jnp.int32).T
    )
    by_group = slot_width.reshape(GROUP_FRAMES, 2, GROUP_FRAMES, SLOTS).transpose(2, 1, 0, 3)
    by_group = by_group.reshape(GROUPS, GROUP_FRAMES, SLOTS)
    needed = jnp.max(by_group, axis=1) > 0
    slots = jnp.arange(SLOTS, dtype=jnp.int32)
    before = (slots[:, None] < slots[None, :]).astype(jnp.int32)
    rank = jnp.dot(needed.astype(jnp.int32), before)
    chosen = needed[:, :, None] & (rank[:, :, None] == slots[None, None, :])
    lists = jnp.sum(jnp.where(chosen, slots[None, :, None], 0), axis=1)
    most = jnp.max(jnp.sum(needed.astype(jnp.int32), axis=1))
    y, x, zh, zl, core = place()
    group = 2 * x + zl
    my_width = lax.dynamic_index_in_dim(by_group, group, 0, False)
    my_rank = lax.dynamic_index_in_dim(rank, group, 0, False)
    own = slots[None, :] == (GROUP_FRAMES * (2 * slots[:GROUP_FRAMES] + zl) + x)[:, None]
    others = (my_width > 0) & jnp.logical_not(own)
    order = jnp.where(own, 0, 1 + jnp.dot(others.astype(jnp.int32), before))
    here = (own | others)[:, :, None] & (order[:, :, None] == slots[None, None, :])
    codes = jnp.sum(jnp.where(here, (my_rank[None, :] * 1024 + my_width)[:, :, None], 0), axis=1)
    counts = 1 + jnp.sum(others.astype(jnp.int32), axis=1)
    info = jnp.concatenate([codes.reshape(-1), counts])

    def run(capacity):
        def branch(lists, info, queries, key_rows, values):
            q_local, keys, vals = gather(capacity, lists, queries, key_rows, values)
            return attend(info, q_local, keys, vals)

        return branch

    index = sum((most > room).astype(jnp.int32) for room in ROOMS[:-1])
    outcome = lax.switch(
        index, [run(room) for room in ROOMS], lists.reshape(-1), info, queries, key_rows, values
    )
    return send_back(outcome)


def solution(mesh):
    placed = (
        P(("rep", "frame", "head"), None),
        P(("rep", "frame", "head"), None),
        P(("rep", "frame", "head"), None),
        P(),
        P(),
    )
    return jax.shard_map(
        on_device,
        mesh=mesh,
        in_specs=placed,
        out_specs=P(("rep", "frame", "head"), None),
        check_vma=False,
    )
```

```python
import functools
import math

import jax
import jax.numpy as jnp
from jax import lax
from jax.experimental import pallas as pl
from jax.experimental.pallas import tpu as pltpu
from jax.sharding import PartitionSpec as P

HEADS = 32
HEAD_DIM = 128
FRAME_PIX = 512
GROUPS = 8
GROUP_FRAMES = 4
CHUNK = 64
SLOTS = 32
ROOMS = (12, 13, 14, 32)
MESH = pl.DeviceIdType.MESH
SCALE = math.log2(math.e) / math.sqrt(HEAD_DIM)


def place():
    y = lax.axis_index("frame")
    xz = lax.axis_index("head")
    x = lax.div(xz, 8)
    z = lax.rem(xz, 8)
    return y, x, lax.div(z, 2), lax.rem(z, 2), lax.axis_index("rep")


def partner(t, y, zh):
    return lax.rem(y + 3 * t, 8), lax.rem(zh + t + lax.div(t, 8), 4)


def send(src, dst, send_sem, recv_sem, here, there):
    same = (here[0] == there[0]) & (here[1] == there[1])

    @pl.when(same)
    def _():
        pltpu.make_async_copy(src, dst, recv_sem).start()

    @pl.when(jnp.logical_not(same))
    def _():
        pltpu.make_async_remote_copy(
            src_ref=src,
            dst_ref=dst,
            send_sem=send_sem,
            recv_sem=recv_sem,
            device_id=there,
            device_id_type=MESH,
        ).start()


def greet(there):
    pl.semaphore_signal(
        pltpu.get_barrier_semaphore(), inc=1, device_id=there, device_id_type=MESH
    )


def wait_bytes(ref, sem):
    pltpu.make_async_copy(ref, ref, sem).wait()


def chunk_of(y, x, zh, zl):
    turn = lax.rem(x + 16 - y - zh, 4)
    return lax.rem(2 * zh + jnp.where(zl == 1, turn + 1, 8 - turn), 8)


def gather_kernel(
    capacity,
    lists_ref,
    q_ref,
    k_ref,
    v_ref,
    q_out,
    k_out,
    v_out,
    k_spread,
    v_spread,
    k_other,
    v_other,
    k_stage,
    v_stage,
    k_relay,
    v_relay,
    send_sem,
    recv_sem,
    relay_sem,
    quarter_sem,
):
    y, x, zh, zl, core = place()
    z = 2 * zh + zl
    here = (y, x * 8 + z, core)
    right, left = lax.rem(x + 1, 4), lax.rem(x + 3, 4)

    def at(x2, zl2):
        return (y, x2 * 8 + 2 * zh + zl2, core)

    chunk = chunk_of(y, x, zh, zl)
    same_chunk = chunk == z
    same_query = lax.rem(y, 2) == zl

    def greet_senders(t, carry):
        y1, x1 = lax.rem(t, 8), lax.div(t, 8)

        @pl.when((y1 != y) | (x1 != x) | (chunk != z))
        def _():
            greet((y1, x1 * 8 + chunk, core))

        y2, z2 = 2 * lax.rem(t, 4) + zl, lax.div(t, 4)

        @pl.when((y2 != y) | (z2 != z))
        def _():
            greet((y2, x * 8 + z2, core))

        return carry

    lax.fori_loop(0, HEADS, greet_senders, 0)
    for mate in (at(right, zl), at(left, zl), at(x, 1 - zl)):
        greet(mate)
    pl.semaphore_wait(
        pltpu.get_barrier_semaphore(),
        2 * HEADS + 3 - same_chunk.astype(jnp.int32) - same_query.astype(jnp.int32),
    )

    def spread(source, landing, number):
        def step(t, carry):
            y2, zh2 = partner(t, y, zh)
            off = lax.rem(z - 2 * zh2 + 11, 8) - 3
            zl2 = (off > 0).astype(jnp.int32)
            turn = jnp.where(off > 0, off - 1, -off)
            x2 = lax.rem(turn + y2 + zh2, 4)
            head = y2 * 4 + zh2
            send(
                source.at[:, pl.ds(pl.multiple_of(head * HEAD_DIM, HEAD_DIM), HEAD_DIM)],
                landing.at[lax.div(t, 4) * 4 + x],
                send_sem.at[number],
                quarter_sem.at[4 * number + lax.div(t, 8)],
                here,
                (y2, x2 * 8 + 2 * zh2 + zl2, core),
            )
            return carry

        lax.fori_loop(0, HEADS, step, 0)

    def send_queries():
        def step(t, carry):
            y2, zh2 = partner(t, y, zh)
            z2 = 2 * zh2 + lax.rem(y, 2)
            head = y2 * 4 + zh2
            send(
                q_ref.at[:, pl.ds(pl.multiple_of(head * HEAD_DIM, HEAD_DIM), HEAD_DIM)],
                q_out.at[lax.div(y, 2), z],
                send_sem.at[2],
                recv_sem.at[2],
                here,
                (y2, x * 8 + z2, core),
            )
            return carry

        lax.fori_loop(0, HEADS, step, 0)

    def remote(src, dst, sent, received, there):
        return pltpu.make_async_remote_copy(
            src_ref=src,
            dst_ref=dst,
            send_sem=sent,
            recv_sem=received,
            device_id=there,
            device_id_type=MESH,
        )

    def swap(spread_ref, other_ref, number):
        for quarter in range(4):
            part = pl.ds(8 * quarter, 8)
            wait_bytes(spread_ref.at[part], quarter_sem.at[4 * number + quarter])
            remote(
                spread_ref.at[part],
                other_ref.at[part],
                send_sem.at[3 + number],
                recv_sem.at[3 + number],
                at(x, 1 - zl),
            ).start()

    middle = capacity // 2
    halves = (
        (pl.ds(0, middle), right, left),
        (pl.ds(middle, capacity - middle), left, right),
    )
    mates = (right, left, lax.rem(x + 2, 4), x)

    def to_mates(side, spread_ref, stage, relay, landing, number):
        def pick(p, carry):
            for mate, x2 in enumerate(mates):
                stage[side, mate, p] = spread_ref[lists_ref[side * 256 + (2 * x2 + zl) * SLOTS + p]]
            return carry

        lax.fori_loop(0, capacity, pick, 0)
        rows = landing.at[:, chunk_of(y, x, zh, zl if side == 0 else 1 - zl)]
        sent, landed = send_sem.at[5 + number], recv_sem.at[5 + number]
        for half, (part, by, _) in enumerate(halves):
            remote(
                stage.at[side, 2, part],
                relay.at[side, part],
                sent,
                relay_sem.at[4 * number + 2 * side + half],
                at(by, zl),
            ).start()
        remote(stage.at[side, 0], rows, sent, landed, at(right, zl)).start()
        remote(stage.at[side, 1], rows, sent, landed, at(left, zl)).start()
        pltpu.make_async_copy(stage.at[side, 3], rows, landed).start()

    def pass_on(side, relay, landing, number):
        for half, (part, there, owner) in enumerate(halves):
            wait_bytes(relay.at[side, part], relay_sem.at[4 * number + 2 * side + half])
            rows = landing.at[part, chunk_of(y, owner, zh, zl if side == 0 else 1 - zl)]
            remote(
                relay.at[side, part], rows, send_sem.at[7 + number], recv_sem.at[5 + number], at(there, zl)
            ).start()

    spread(k_ref, k_spread, 0)
    spread(v_ref, v_spread, 1)
    swap(k_spread, k_other, 0)
    to_mates(0, k_spread, k_stage, k_relay, k_out, 0)
    send_queries()
    swap(v_spread, v_other, 1)
    to_mates(0, v_spread, v_stage, v_relay, v_out, 1)
    wait_bytes(k_other, recv_sem.at[3])
    to_mates(1, k_other, k_stage, k_relay, k_out, 0)
    pass_on(0, k_relay, k_out, 0)
    wait_bytes(v_other, recv_sem.at[4])
    to_mates(1, v_other, v_stage, v_relay, v_out, 1)
    pass_on(0, v_relay, v_out, 1)
    pass_on(1, k_relay, k_out, 0)
    pass_on(1, v_relay, v_out, 1)
    wait_bytes(k_spread, send_sem.at[3])
    wait_bytes(v_spread, send_sem.at[4])

    def wait_sent(number, own_copy):
        @pl.when(own_copy)
        def _():
            wait_bytes(k_ref.at[:, pl.ds(0, (HEADS - 1) * HEAD_DIM)], send_sem.at[number])

        @pl.when(jnp.logical_not(own_copy))
        def _():
            wait_bytes(k_spread, send_sem.at[number])

    own_copy = same_chunk & (lax.rem(y + zh, 4) == x)
    wait_sent(0, own_copy)
    wait_sent(1, own_copy)
    wait_sent(2, same_query)
    for number, stage, relay in ((0, k_stage, k_relay), (1, v_stage, v_relay)):
        wait_bytes(stage.at[:, pl.ds(0, 3)], send_sem.at[5 + number])
        wait_bytes(relay, send_sem.at[7 + number])
    wait_bytes(q_out, recv_sem.at[2])
    wait_bytes(k_out, recv_sem.at[5])
    wait_bytes(v_out, recv_sem.at[6])


def gather(capacity, lists, queries, key_rows, values):
    any_space = pl.BlockSpec(memory_space=pl.ANY)
    pieces = (GROUP_FRAMES, GROUPS, CHUNK, HEAD_DIM)
    picked = (capacity, GROUPS, CHUNK, HEAD_DIM)
    scratch = [(SLOTS,)] * 4 + [(2, 4, capacity)] * 2 + [(2, capacity)] * 2
    return pl.pallas_call(
        functools.partial(gather_kernel, capacity),
        out_shape=[jax.ShapeDtypeStruct(shape, jnp.bfloat16) for shape in (pieces, picked, picked)],
        in_specs=[pl.BlockSpec(memory_space=pltpu.SMEM), any_space, any_space, any_space],
        out_specs=[any_space] * 3,
        scratch_shapes=[
            *(pltpu.VMEM((*shape, CHUNK, HEAD_DIM), jnp.bfloat16) for shape in scratch),
            pltpu.SemaphoreType.DMA((9,)),
            pltpu.SemaphoreType.DMA((7,)),
            pltpu.SemaphoreType.DMA((8,)),
            pltpu.SemaphoreType.DMA((8,)),
        ],
        compiler_params=pltpu.CompilerParams(
            collective_id=ROOMS.index(capacity), has_side_effects=True, vmem_limit_bytes=40 * 2**20
        ),
    )(lists, queries, key_rows, values)


BLOCK = 128


def attend_kernel(info_ref, q_ref, k_ref, v_ref, o_ref, apart, ones, top, weighted):
    square = (FRAME_PIX, FRAME_PIX)
    apart[...] = jnp.abs(
        lax.broadcasted_iota(jnp.int32, square, 0) - lax.broadcasted_iota(jnp.int32, square, 1)
    )
    ones[...] = jnp.ones_like(ones)

    def tile(own, position, width, first, reach):
        for block in range(FRAME_PIX // BLOCK):
            rows = pl.ds(block * BLOCK, BLOCK)
            low = max(0, block * BLOCK - reach)
            near = pl.ds(low, min(FRAME_PIX, (block + 1) * BLOCK + reach) - low)
            scores = lax.dot_general(
                q_ref[own, rows, :],
                k_ref[position, near, :],
                (((1,), (1,)), ((), ())),
                preferred_element_type=jnp.float32,
            )
            masked = jnp.where(apart[rows, near] < width, scores * SCALE, -1e30)
            high = jnp.max(masked, axis=1, keepdims=True)
            if first:
                new_top = high
            else:
                old_top = top[rows, :]
                new_top = jnp.maximum(old_top, high)
            weight = jnp.exp2(masked - new_top)
            product = jnp.dot(
                weight.astype(jnp.bfloat16),
                jnp.concatenate([v_ref[position, near, :], ones[near, :]], axis=1),
                preferred_element_type=jnp.float32,
            )
            if first:
                weighted[rows, :] = product
            else:
                weighted[rows, :] = weighted[rows, :] * jnp.exp2(old_top - new_top) + product
            top[rows, :] = new_top

    def one_frame(own, carry):
        code = info_ref[own * SLOTS]
        tile(own, lax.shift_right_logical(code, 10), lax.bitwise_and(code, 1023), True, FRAME_PIX)

        def visit(number, inner):
            code = info_ref[own * SLOTS + number]
            position, width = lax.shift_right_logical(code, 10), lax.bitwise_and(code, 1023)

            @pl.when(width > 256)
            def _():
                tile(own, position, width, False, FRAME_PIX)

            @pl.when((width > 128) & (width <= 256))
            def _():
                tile(own, position, width, False, 256)

            @pl.when(width <= 128)
            def _():
                tile(own, position, width, False, 128)

            return inner

        lax.fori_loop(1, info_ref[GROUP_FRAMES * SLOTS + own], visit, 0)
        o_ref[own] = (weighted[:, :HEAD_DIM] / weighted[:, HEAD_DIM:]).astype(jnp.bfloat16)
        return carry

    lax.fori_loop(0, GROUP_FRAMES, one_frame, 0)


def attend(info, q_local, keys, vals):
    capacity = keys.shape[0]
    vmem = pl.BlockSpec(memory_space=pltpu.VMEM)
    outcome = pl.pallas_call(
        attend_kernel,
        out_shape=jax.ShapeDtypeStruct((GROUP_FRAMES, FRAME_PIX, HEAD_DIM), jnp.bfloat16),
        in_specs=[pl.BlockSpec(memory_space=pltpu.SMEM), vmem, vmem, vmem],
        out_specs=vmem,
        scratch_shapes=[
            pltpu.VMEM((FRAME_PIX, FRAME_PIX), jnp.int32),
            pltpu.VMEM((FRAME_PIX, HEAD_DIM), jnp.bfloat16),
            pltpu.VMEM((FRAME_PIX, 1), jnp.float32),
            pltpu.VMEM((FRAME_PIX, 2 * HEAD_DIM), jnp.float32),
        ],
        compiler_params=pltpu.CompilerParams(vmem_limit_bytes=40 * 2**20),
    )(
        info,
        q_local.reshape(GROUP_FRAMES, FRAME_PIX, HEAD_DIM),
        keys.reshape(capacity, FRAME_PIX, HEAD_DIM),
        vals.reshape(capacity, FRAME_PIX, HEAD_DIM),
    )
    return outcome.reshape(GROUP_FRAMES, GROUPS, CHUNK, HEAD_DIM)


def return_kernel(o_ref, out_ref, send_sem, recv_sem):
    y, x, zh, zl, core = place()
    z = 2 * zh + zl
    here = (y, x * 8 + z, core)
    head = y * 4 + zh
    same = lax.rem(y, 2) == zl

    def greet_senders(t, carry):
        y2, z2 = lax.rem(t, 8), 2 * lax.div(t, 8) + lax.rem(y, 2)

        @pl.when((y2 != y) | (z2 != z))
        def _():
            greet((y2, x * 8 + z2, core))

        return carry

    lax.fori_loop(0, HEADS, greet_senders, 0)
    pl.semaphore_wait(pltpu.get_barrier_semaphore(), HEADS - same.astype(jnp.int32))

    def step(t, carry):
        number = lax.rem(lax.div(y, 2) + t + lax.div(t, 8), 4)
        y2 = 2 * number + zl
        z2 = lax.rem(z + 3 * t, 8)
        send(
            o_ref.at[number, z2],
            out_ref.at[head],
            send_sem,
            recv_sem,
            here,
            (y2, x * 8 + z2, core),
        )
        return carry

    lax.fori_loop(0, HEADS, step, 0)
    sent = out_ref.at[pl.ds(0, HEADS - 1)]

    @pl.when(same)
    def _():
        wait_bytes(sent, send_sem)

    @pl.when(jnp.logical_not(same))
    def _():
        wait_bytes(out_ref, send_sem)

    wait_bytes(out_ref, recv_sem)


def send_back(outcome):
    any_space = pl.BlockSpec(memory_space=pl.ANY)
    by_head = pl.pallas_call(
        return_kernel,
        out_shape=jax.ShapeDtypeStruct((HEADS, CHUNK, HEAD_DIM), jnp.bfloat16),
        in_specs=[any_space],
        out_specs=any_space,
        scratch_shapes=[pltpu.SemaphoreType.DMA, pltpu.SemaphoreType.DMA],
        compiler_params=pltpu.CompilerParams(collective_id=len(ROOMS), has_side_effects=True),
    )(outcome)
    return by_head.transpose(1, 0, 2).reshape(CHUNK, HEADS * HEAD_DIM)


def plan_kernel(slot_ref, tiles_ref, lists_ref, info_ref, index_ref):
    y, x, zh, zl, core = place()
    half, single = jnp.bfloat16, jnp.float32

    def flags(condition):
        return jnp.where(condition, 1.0, 0.0)

    def times(left, right):
        return jnp.dot(left.astype(half), right.astype(half), preferred_element_type=single)

    def across(left, right):
        return lax.dot_general(
            left.astype(half), right.astype(half), (((1,), (1,)), ((), ())), preferred_element_type=single
        )

    def iota(rows, columns, dimension):
        return lax.broadcasted_iota(jnp.int32, (rows, columns), dimension)

    diagonal = iota(SLOTS, SLOTS, 0) == iota(SLOTS, SLOTS, 1)
    slots = jnp.sum(jnp.where(diagonal, slot_ref[...], 0), axis=1, keepdims=True)
    on_query = tiles_ref[0:1, :] == slots
    on_key = flags(tiles_ref[1:2, :] == slots)
    widths = tiles_ref[2:3, :]
    coarse = across(jnp.where(on_query, lax.shift_right_logical(widths, 4).astype(single), 0.0), on_key)
    fine = across(jnp.where(on_query, lax.bitwise_and(widths, 15).astype(single), 0.0), on_key)
    slot = iota(GROUPS, SLOTS, 1)
    group = 2 * lax.bitwise_and(slot, 3) + lax.bitwise_and(lax.shift_right_logical(slot, 2), 1)
    in_group = flags(group == iota(GROUPS, SLOTS, 0))
    needed = flags(times(in_group, flags(coarse + fine > 0)) > 0)
    before = flags(iota(SLOTS, SLOTS, 0) < iota(SLOTS, SLOTS, 1))
    rank = times(needed, before)
    order = iota(SLOTS, SLOTS, 0).astype(single)
    picks = [
        flags(rank[g : g + 1] == order) * needed[g : g + 1] for g in range(GROUPS)
    ]
    number = iota(1, SLOTS, 1)
    for side, low in ((0, zl), (1, 1 - zl)):
        source = lax.div(chunk_of(y, x, zh, low), 2)
        eighth = lax.bitwise_and(3 * (y + 8 - lax.shift_right_logical(number, 2)), 7)
        quarter = lax.bitwise_and(zh + 12 - source - eighth, 3)
        spot = quarter * 8 + lax.bitwise_and(eighth, 4) + lax.bitwise_and(number, 3)
        found = across(spot.astype(single), jnp.concatenate(picks, axis=0))
        lists_ref[:, side * 256 : side * 256 + 256] = found.astype(jnp.int32)
    most = jnp.max(jnp.sum(needed, axis=1, keepdims=True), axis=0, keepdims=True)
    index = sum(flags(most > room) for room in ROOMS[:-1])
    index_ref[...] = jnp.broadcast_to(index, (1, 128)).astype(jnp.int32)
    query = iota(GROUP_FRAMES, SLOTS, 0)
    own = flags(iota(GROUP_FRAMES, SLOTS, 1) == GROUP_FRAMES * (2 * query + zl) + x)
    my_coarse, my_fine = times(own, coarse), times(own, fine)
    others = flags(my_coarse + my_fine > 0) * (1.0 - own)
    turn = (1.0 + times(others, before)) * (1.0 - own)
    at = [
        flags(turn[q : q + 1] == order) * (own + others)[q : q + 1] for q in range(GROUP_FRAMES)
    ]
    ones = jnp.ones((1, SLOTS), single)
    my_rank = times(flags(iota(1, GROUPS, 1) == 2 * x + zl), rank)
    place_of = across(my_rank, jnp.concatenate(at, axis=0))
    coarse_of = across(
        ones, jnp.concatenate([at[q] * my_coarse[q : q + 1] for q in range(GROUP_FRAMES)], axis=0)
    )
    fine_of = across(
        ones, jnp.concatenate([at[q] * my_fine[q : q + 1] for q in range(GROUP_FRAMES)], axis=0)
    )
    info_ref[:, :128] = (place_of * 1024 + coarse_of * 16 + fine_of).astype(jnp.int32)
    padded = jnp.concatenate([others, jnp.zeros((128 - GROUP_FRAMES, SLOTS), single)], axis=0)
    info_ref[:, 128:] = 1 + across(ones, padded).astype(jnp.int32)


def plan(slot_frame, radial_tiles):
    vmem = pl.BlockSpec(memory_space=pltpu.VMEM)
    lists, info, index = pl.pallas_call(
        plan_kernel,
        out_shape=[jax.ShapeDtypeStruct((1, size), jnp.int32) for size in (512, 256, 128)],
        in_specs=[vmem] * 2,
        out_specs=[vmem] * 3,
    )(slot_frame.reshape(1, SLOTS), radial_tiles.T)
    return lists.reshape(-1), info.reshape(-1), index[0, 0]


def on_device(queries, key_rows, values, slot_frame, radial_tiles):
    lists, info, index = plan(slot_frame, radial_tiles)

    def run(capacity):
        def branch(lists, info, queries, key_rows, values):
            q_local, keys, vals = gather(capacity, lists, queries, key_rows, values)
            return attend(info, q_local, keys, vals)

        return branch

    outcome = lax.switch(
        index, [run(room) for room in ROOMS], lists, info, queries, key_rows, values
    )
    return send_back(outcome)


def solution(mesh):
    placed = (
        P(("rep", "frame", "head"), None),
        P(("rep", "frame", "head"), None),
        P(("rep", "frame", "head"), None),
        P(),
        P(),
    )
    return jax.shard_map(
        on_device,
        mesh=mesh,
        in_specs=placed,
        out_specs=P(("rep", "frame", "head"), None),
        check_vma=False,
    )
```

```python
import functools
import math

import jax
import jax.numpy as jnp
from jax import lax
from jax.experimental import pallas as pl
from jax.experimental.pallas import tpu as pltpu
from jax.sharding import PartitionSpec as P

HEADS = 32
HEAD_DIM = 128
FRAME_PIX = 512
GROUPS = 8
GROUP_FRAMES = 4
CHUNK = 64
SLOTS = 32
ROOMS = (12, 13, 14, 32)
MESH = pl.DeviceIdType.MESH
SCALE = math.log2(math.e) / math.sqrt(HEAD_DIM)


def place():
    y = lax.axis_index("frame")
    xz = lax.axis_index("head")
    x = lax.div(xz, 8)
    z = lax.rem(xz, 8)
    return y, x, lax.div(z, 2), lax.rem(z, 2), lax.axis_index("rep")


def remote(src, dst, sent, received, there):
    return pltpu.make_async_remote_copy(
        src_ref=src,
        dst_ref=dst,
        send_sem=sent,
        recv_sem=received,
        device_id=there,
        device_id_type=MESH,
    )


def send(src, dst, sent, received, here, there):
    same = (here[0] == there[0]) & (here[1] == there[1])

    @pl.when(same)
    def _():
        pltpu.make_async_copy(src, dst, received).start()

    @pl.when(jnp.logical_not(same))
    def _():
        remote(src, dst, sent, received, there).start()


def greet(there):
    pl.semaphore_signal(
        pltpu.get_barrier_semaphore(), inc=1, device_id=there, device_id_type=MESH
    )


def wait_bytes(ref, sem):
    pltpu.make_async_copy(ref, ref, sem).wait()


def chunk_of(y, x, zh, zl):
    turn = lax.rem(x + 16 - y - zh, 4)
    return lax.rem(2 * zh + jnp.where(zl == 1, turn + 1, 8 - turn), 8)


def gather_kernel(
    capacity,
    lists_ref,
    q_ref,
    k_ref,
    v_ref,
    q_out,
    k_out,
    v_out,
    k_spread,
    v_spread,
    k_other,
    v_other,
    k_stage,
    v_stage,
    k_relay,
    v_relay,
    send_sem,
    recv_sem,
    relay_sem,
    quarter_sem,
):
    y, x, zh, zl, core = place()
    z = 2 * zh + zl
    here = (y, x * 8 + z, core)
    right, left = lax.rem(x + 1, 4), lax.rem(x + 3, 4)

    def at(x2, zl2):
        return (y, x2 * 8 + 2 * zh + zl2, core)

    chunk = chunk_of(y, x, zh, zl)
    same_chunk = chunk == z
    same_query = lax.rem(y, 2) == zl

    xs = [lax.rem(x + dx, 4) * 8 + chunk for dx in range(4)]
    ys = [2 * number + zl for number in range(4)]

    def greet_senders(i, carry):
        y1, xz1 = lax.rem(y + i, 8), x * 8 + lax.rem(z + i, 8)
        for xz in xs:
            greet((y1, xz, core))
        for y2 in ys:
            greet((y2, xz1, core))
        return carry

    lax.fori_loop(1, 8, greet_senders, 0)
    for xz in xs[1:]:
        greet((y, xz, core))

    @pl.when(jnp.logical_not(same_chunk))
    def _():
        greet((y, xs[0], core))

    for y2 in ys:

        @pl.when(y2 != y)
        def _(y2=y2):
            greet((y2, x * 8 + z, core))

    for mate in (at(right, zl), at(left, zl), at(x, 1 - zl)):
        greet(mate)
    pl.semaphore_wait(
        pltpu.get_barrier_semaphore(),
        2 * HEADS + 3 - same_chunk.astype(jnp.int32) - same_query.astype(jnp.int32),
    )

    planes = [lax.rem(y + 3 * e, 8) for e in range(8)]
    own_copy = same_chunk

    def columns(source, head):
        return source.at[:, pl.ds(pl.multiple_of(head * HEAD_DIM, HEAD_DIM), HEAD_DIM)]

    def spread(source, landing, number):
        def step(quarter, carry):
            zhs = [lax.rem(zh + quarter + r, 4) for r in range(4)]
            offs = [lax.rem(z - 2 * zh2 + 11, 8) - 3 for zh2 in zhs]
            lows = [2 * zh2 + (off > 0).astype(jnp.int32) for zh2, off in zip(zhs, offs)]
            turns = [jnp.where(off > 0, off - 1, -off) + zh2 for off, zh2 in zip(offs, zhs)]
            sent, received = send_sem.at[number], quarter_sem.at[4 * number + quarter]
            for e, y2 in enumerate(planes):
                piece = columns(source, y2 * 4 + zhs[e % 4])
                rows = landing.at[8 * quarter + e // 4 * 4 + x]
                there = (y2, lax.rem(turns[e % 4] + y2, 4) * 8 + lows[e % 4], core)
                if e == 0:
                    send(piece, rows, sent, received, here, there)
                else:
                    remote(piece, rows, sent, received, there).start()
            return carry

        lax.fori_loop(0, 4, step, 0)

    def send_queries():
        rows = q_out.at[lax.div(y, 2), z]
        odd = x * 8 + lax.rem(y, 2)

        def step(quarter, carry):
            zhs = [lax.rem(zh + quarter + r, 4) for r in range(4)]
            for e, y2 in enumerate(planes):
                piece = columns(q_ref, y2 * 4 + zhs[e % 4])
                there = (y2, 2 * zhs[e % 4] + odd, core)
                if e == 0:
                    send(piece, rows, send_sem.at[2], recv_sem.at[2], here, there)
                else:
                    remote(piece, rows, send_sem.at[2], recv_sem.at[2], there).start()
            return carry

        lax.fori_loop(0, 4, step, 0)

    def swap(spread_ref, other_ref, number):
        for quarter in range(4):
            part = pl.ds(8 * quarter, 8)
            wait_bytes(spread_ref.at[part], quarter_sem.at[4 * number + quarter])
            remote(
                spread_ref.at[part],
                other_ref.at[part],
                send_sem.at[3 + number],
                recv_sem.at[3 + number],
                at(x, 1 - zl),
            ).start()

    middle = capacity // 2
    halves = (
        (pl.ds(0, middle), right, left),
        (pl.ds(middle, capacity - middle), left, right),
    )
    mates = (right, left, lax.rem(x + 2, 4), x)
    bases = [(2 * x2 + zl) * SLOTS for x2 in mates]

    def to_mates(side, spread_ref, stage, relay, landing, number):
        def pick(p, carry):
            for mate, base in enumerate(bases):
                stage[side, mate, p] = spread_ref[lists_ref[side * 256 + base + p]]
            return carry

        lax.fori_loop(0, capacity, pick, 0)
        rows = landing.at[:, chunk_of(y, x, zh, zl if side == 0 else 1 - zl)]
        sent, landed = send_sem.at[5 + number], recv_sem.at[5 + number]
        for half, (part, by, _) in enumerate(halves):
            remote(
                stage.at[side, 2, part],
                relay.at[side, part],
                sent,
                relay_sem.at[4 * number + 2 * side + half],
                at(by, zl),
            ).start()
        remote(stage.at[side, 0], rows, sent, landed, at(right, zl)).start()
        remote(stage.at[side, 1], rows, sent, landed, at(left, zl)).start()
        pltpu.make_async_copy(stage.at[side, 3], rows, landed).start()

    def pass_on(side, relay, landing, number):
        for half, (part, there, owner) in enumerate(halves):
            wait_bytes(relay.at[side, part], relay_sem.at[4 * number + 2 * side + half])
            rows = landing.at[part, chunk_of(y, owner, zh, zl if side == 0 else 1 - zl)]
            remote(
                relay.at[side, part], rows, send_sem.at[7 + number], recv_sem.at[5 + number], at(there, zl)
            ).start()

    spread(k_ref, k_spread, 0)
    spread(v_ref, v_spread, 1)
    swap(k_spread, k_other, 0)
    to_mates(0, k_spread, k_stage, k_relay, k_out, 0)
    send_queries()
    swap(v_spread, v_other, 1)
    to_mates(0, v_spread, v_stage, v_relay, v_out, 1)
    wait_bytes(k_other, recv_sem.at[3])
    to_mates(1, k_other, k_stage, k_relay, k_out, 0)
    pass_on(0, k_relay, k_out, 0)
    wait_bytes(v_other, recv_sem.at[4])
    to_mates(1, v_other, v_stage, v_relay, v_out, 1)
    pass_on(0, v_relay, v_out, 1)
    pass_on(1, k_relay, k_out, 0)
    pass_on(1, v_relay, v_out, 1)
    wait_bytes(k_spread, send_sem.at[3])
    wait_bytes(v_spread, send_sem.at[4])

    def wait_sent(number, own_copy):
        @pl.when(own_copy)
        def _():
            wait_bytes(k_ref.at[:, pl.ds(0, (HEADS - 1) * HEAD_DIM)], send_sem.at[number])

        @pl.when(jnp.logical_not(own_copy))
        def _():
            wait_bytes(k_spread, send_sem.at[number])

    wait_sent(0, own_copy)
    wait_sent(1, own_copy)
    wait_sent(2, same_query)
    for number, stage, relay in ((0, k_stage, k_relay), (1, v_stage, v_relay)):
        wait_bytes(stage.at[:, pl.ds(0, 3)], send_sem.at[5 + number])
        wait_bytes(relay, send_sem.at[7 + number])
    wait_bytes(q_out, recv_sem.at[2])
    wait_bytes(k_out, recv_sem.at[5])
    wait_bytes(v_out, recv_sem.at[6])


def gather(capacity, lists, queries, key_rows, values):
    any_space = pl.BlockSpec(memory_space=pl.ANY)
    pieces = (GROUP_FRAMES, GROUPS, CHUNK, HEAD_DIM)
    picked = (capacity, GROUPS, CHUNK, HEAD_DIM)
    scratch = [(SLOTS,)] * 4 + [(2, 4, capacity)] * 2 + [(2, capacity)] * 2
    return pl.pallas_call(
        functools.partial(gather_kernel, capacity),
        out_shape=[jax.ShapeDtypeStruct(shape, jnp.bfloat16) for shape in (pieces, picked, picked)],
        in_specs=[pl.BlockSpec(memory_space=pltpu.SMEM), any_space, any_space, any_space],
        out_specs=[any_space] * 3,
        scratch_shapes=[
            *(pltpu.VMEM((*shape, CHUNK, HEAD_DIM), jnp.bfloat16) for shape in scratch),
            pltpu.SemaphoreType.DMA((9,)),
            pltpu.SemaphoreType.DMA((7,)),
            pltpu.SemaphoreType.DMA((8,)),
            pltpu.SemaphoreType.DMA((8,)),
        ],
        compiler_params=pltpu.CompilerParams(
            collective_id=ROOMS.index(capacity), has_side_effects=True, vmem_limit_bytes=40 * 2**20
        ),
    )(lists, queries, key_rows, values)


BLOCK = 128


def attend_kernel(info_ref, q_ref, k_ref, v_ref, o_ref, apart, ones, top, weighted):
    square = (FRAME_PIX, FRAME_PIX)
    apart[...] = jnp.abs(
        lax.broadcasted_iota(jnp.int32, square, 0) - lax.broadcasted_iota(jnp.int32, square, 1)
    )
    ones[...] = jnp.ones_like(ones)

    def tile(own, position, width, first, reach):
        for block in range(FRAME_PIX // BLOCK):
            rows = pl.ds(block * BLOCK, BLOCK)
            low = max(0, block * BLOCK - reach)
            near = pl.ds(low, min(FRAME_PIX, (block + 1) * BLOCK + reach) - low)
            scores = lax.dot_general(
                q_ref[own, rows, :],
                k_ref[position, near, :],
                (((1,), (1,)), ((), ())),
                preferred_element_type=jnp.float32,
            )
            masked = jnp.where(apart[rows, near] < width, scores * SCALE, -1e30)
            high = jnp.max(masked, axis=1, keepdims=True)
            if first:
                new_top = high
            else:
                old_top = top[rows, :]
                new_top = jnp.maximum(old_top, high)
            weight = jnp.exp2(masked - new_top)
            product = jnp.dot(
                weight.astype(jnp.bfloat16),
                jnp.concatenate([v_ref[position, near, :], ones[near, :]], axis=1),
                preferred_element_type=jnp.float32,
            )
            if first:
                weighted[rows, :] = product
            else:
                weighted[rows, :] = weighted[rows, :] * jnp.exp2(old_top - new_top) + product
            top[rows, :] = new_top

    def one_frame(own, carry):
        code = info_ref[own * SLOTS]
        tile(own, lax.shift_right_logical(code, 10), lax.bitwise_and(code, 1023), True, FRAME_PIX)

        def visit(number, inner):
            code = info_ref[own * SLOTS + number]
            position, width = lax.shift_right_logical(code, 10), lax.bitwise_and(code, 1023)

            @pl.when(width > 256)
            def _():
                tile(own, position, width, False, FRAME_PIX)

            @pl.when((width > 128) & (width <= 256))
            def _():
                tile(own, position, width, False, 256)

            @pl.when(width <= 128)
            def _():
                tile(own, position, width, False, 128)

            return inner

        lax.fori_loop(1, info_ref[GROUP_FRAMES * SLOTS + own], visit, 0)
        o_ref[own] = (weighted[:, :HEAD_DIM] / weighted[:, HEAD_DIM:]).astype(jnp.bfloat16)
        return carry

    lax.fori_loop(0, GROUP_FRAMES, one_frame, 0)


def attend(info, q_local, keys, vals):
    capacity = keys.shape[0]
    vmem = pl.BlockSpec(memory_space=pltpu.VMEM)
    outcome = pl.pallas_call(
        attend_kernel,
        out_shape=jax.ShapeDtypeStruct((GROUP_FRAMES, FRAME_PIX, HEAD_DIM), jnp.bfloat16),
        in_specs=[pl.BlockSpec(memory_space=pltpu.SMEM), vmem, vmem, vmem],
        out_specs=vmem,
        scratch_shapes=[
            pltpu.VMEM((FRAME_PIX, FRAME_PIX), jnp.int32),
            pltpu.VMEM((FRAME_PIX, HEAD_DIM), jnp.bfloat16),
            pltpu.VMEM((FRAME_PIX, 1), jnp.float32),
            pltpu.VMEM((FRAME_PIX, 2 * HEAD_DIM), jnp.float32),
        ],
        compiler_params=pltpu.CompilerParams(vmem_limit_bytes=40 * 2**20),
    )(
        info,
        q_local.reshape(GROUP_FRAMES, FRAME_PIX, HEAD_DIM),
        keys.reshape(capacity, FRAME_PIX, HEAD_DIM),
        vals.reshape(capacity, FRAME_PIX, HEAD_DIM),
    )
    return outcome.reshape(GROUP_FRAMES, GROUPS, CHUNK, HEAD_DIM)


def return_kernel(o_ref, out_ref, send_sem, recv_sem):
    y, x, zh, zl, core = place()
    z = 2 * zh + zl
    here = (y, x * 8 + z, core)
    head = y * 4 + zh
    same = lax.rem(y, 2) == zl

    zs = [x * 8 + 2 * number + lax.rem(y, 2) for number in range(4)]

    def greet_senders(i, carry):
        y1 = lax.rem(y + i, 8)
        for xz in zs:
            greet((y1, xz, core))
        return carry

    lax.fori_loop(1, 8, greet_senders, 0)
    for xz in zs:

        @pl.when(xz != x * 8 + z)
        def _(xz=xz):
            greet((y, xz, core))

    pl.semaphore_wait(pltpu.get_barrier_semaphore(), HEADS - same.astype(jnp.int32))
    places = [lax.rem(z + 3 * e, 8) for e in range(8)]
    rows = out_ref.at[head]

    def step(quarter, carry):
        numbers = [lax.rem(lax.div(y, 2) + quarter + r, 4) for r in range(4)]
        for e, z2 in enumerate(places):
            number = numbers[e % 4]
            piece, there = o_ref.at[number, z2], (2 * number + zl, x * 8 + z2, core)
            if e == 0:
                send(piece, rows, send_sem, recv_sem, here, there)
            else:
                remote(piece, rows, send_sem, recv_sem, there).start()
        return carry

    lax.fori_loop(0, 4, step, 0)
    sent = out_ref.at[pl.ds(0, HEADS - 1)]

    @pl.when(same)
    def _():
        wait_bytes(sent, send_sem)

    @pl.when(jnp.logical_not(same))
    def _():
        wait_bytes(out_ref, send_sem)

    wait_bytes(out_ref, recv_sem)


def send_back(outcome):
    any_space = pl.BlockSpec(memory_space=pl.ANY)
    by_head = pl.pallas_call(
        return_kernel,
        out_shape=jax.ShapeDtypeStruct((HEADS, CHUNK, HEAD_DIM), jnp.bfloat16),
        in_specs=[any_space],
        out_specs=any_space,
        scratch_shapes=[pltpu.SemaphoreType.DMA, pltpu.SemaphoreType.DMA],
        compiler_params=pltpu.CompilerParams(collective_id=len(ROOMS), has_side_effects=True),
    )(outcome)
    return by_head.transpose(1, 0, 2).reshape(CHUNK, HEADS * HEAD_DIM)


def plan_kernel(slot_ref, tiles_ref, lists_ref, info_ref, index_ref):
    y, x, zh, zl, core = place()
    half, single = jnp.bfloat16, jnp.float32

    def flags(condition):
        return jnp.where(condition, 1.0, 0.0)

    def times(left, right):
        return jnp.dot(left.astype(half), right.astype(half), preferred_element_type=single)

    def across(left, right):
        return lax.dot_general(
            left.astype(half), right.astype(half), (((1,), (1,)), ((), ())), preferred_element_type=single
        )

    def iota(rows, columns, dimension):
        return lax.broadcasted_iota(jnp.int32, (rows, columns), dimension)

    diagonal = iota(SLOTS, SLOTS, 0) == iota(SLOTS, SLOTS, 1)
    slots = jnp.sum(jnp.where(diagonal, slot_ref[...], 0), axis=1, keepdims=True)
    on_query = tiles_ref[0:1, :] == slots
    on_key = flags(tiles_ref[1:2, :] == slots)
    widths = tiles_ref[2:3, :]
    coarse = across(jnp.where(on_query, lax.shift_right_logical(widths, 4).astype(single), 0.0), on_key)
    fine = across(jnp.where(on_query, lax.bitwise_and(widths, 15).astype(single), 0.0), on_key)
    slot = iota(GROUPS, SLOTS, 1)
    group = 2 * lax.bitwise_and(slot, 3) + lax.bitwise_and(lax.shift_right_logical(slot, 2), 1)
    in_group = flags(group == iota(GROUPS, SLOTS, 0))
    needed = flags(times(in_group, flags(coarse + fine > 0)) > 0)
    before = flags(iota(SLOTS, SLOTS, 0) < iota(SLOTS, SLOTS, 1))
    rank = times(needed, before)
    order = iota(SLOTS, SLOTS, 0).astype(single)
    picks = [
        flags(rank[g : g + 1] == order) * needed[g : g + 1] for g in range(GROUPS)
    ]
    number = iota(1, SLOTS, 1)
    for side, low in ((0, zl), (1, 1 - zl)):
        source = lax.div(chunk_of(y, x, zh, low), 2)
        eighth = lax.bitwise_and(3 * (y + 8 - lax.shift_right_logical(number, 2)), 7)
        quarter = lax.bitwise_and(zh + 12 - source - eighth, 3)
        spot = quarter * 8 + lax.bitwise_and(eighth, 4) + lax.bitwise_and(number, 3)
        found = across(spot.astype(single), jnp.concatenate(picks, axis=0))
        lists_ref[:, side * 256 : side * 256 + 256] = found.astype(jnp.int32)
    most = jnp.max(jnp.sum(needed, axis=1, keepdims=True), axis=0, keepdims=True)
    index = sum(flags(most > room) for room in ROOMS[:-1])
    index_ref[...] = jnp.broadcast_to(index, (1, 128)).astype(jnp.int32)
    query = iota(GROUP_FRAMES, SLOTS, 0)
    own = flags(iota(GROUP_FRAMES, SLOTS, 1) == GROUP_FRAMES * (2 * query + zl) + x)
    my_coarse, my_fine = times(own, coarse), times(own, fine)
    others = flags(my_coarse + my_fine > 0) * (1.0 - own)
    turn = (1.0 + times(others, before)) * (1.0 - own)
    at = [
        flags(turn[q : q + 1] == order) * (own + others)[q : q + 1] for q in range(GROUP_FRAMES)
    ]
    ones = jnp.ones((1, SLOTS), single)
    my_rank = times(flags(iota(1, GROUPS, 1) == 2 * x + zl), rank)
    place_of = across(my_rank, jnp.concatenate(at, axis=0))
    coarse_of = across(
        ones, jnp.concatenate([at[q] * my_coarse[q : q + 1] for q in range(GROUP_FRAMES)], axis=0)
    )
    fine_of = across(
        ones, jnp.concatenate([at[q] * my_fine[q : q + 1] for q in range(GROUP_FRAMES)], axis=0)
    )
    info_ref[:, :128] = (place_of * 1024 + coarse_of * 16 + fine_of).astype(jnp.int32)
    padded = jnp.concatenate([others, jnp.zeros((128 - GROUP_FRAMES, SLOTS), single)], axis=0)
    info_ref[:, 128:] = 1 + across(ones, padded).astype(jnp.int32)


def plan(slot_frame, radial_tiles):
    vmem = pl.BlockSpec(memory_space=pltpu.VMEM)
    lists, info, index = pl.pallas_call(
        plan_kernel,
        out_shape=[jax.ShapeDtypeStruct((1, size), jnp.int32) for size in (512, 256, 128)],
        in_specs=[vmem] * 2,
        out_specs=[vmem] * 3,
    )(slot_frame.reshape(1, SLOTS), radial_tiles.T)
    return lists.reshape(-1), info.reshape(-1), index[0, 0]


def on_device(queries, key_rows, values, slot_frame, radial_tiles):
    lists, info, index = plan(slot_frame, radial_tiles)

    def run(capacity):
        def branch(lists, info, queries, key_rows, values):
            q_local, keys, vals = gather(capacity, lists, queries, key_rows, values)
            return attend(info, q_local, keys, vals)

        return branch

    outcome = lax.switch(
        index, [run(room) for room in ROOMS], lists, info, queries, key_rows, values
    )
    return send_back(outcome)


def solution(mesh):
    placed = (
        P(("rep", "frame", "head"), None),
        P(("rep", "frame", "head"), None),
        P(("rep", "frame", "head"), None),
        P(),
        P(),
    )
    return jax.shard_map(
        on_device,
        mesh=mesh,
        in_specs=placed,
        out_specs=P(("rep", "frame", "head"), None),
        check_vma=False,
    )
```

```python
import functools
import math

import jax
import jax.numpy as jnp
from jax import lax
from jax.experimental import pallas as pl
from jax.experimental.pallas import tpu as pltpu
from jax.sharding import PartitionSpec as P

HEADS = 32
HEAD_DIM = 128
FRAME_PIX = 512
GROUPS = 8
GROUP_FRAMES = 4
CHUNK = 64
SLOTS = 32
ROOMS = (12, 13, 14, 16, 32)
MESH = pl.DeviceIdType.MESH
SCALE = math.log2(math.e) / math.sqrt(HEAD_DIM)


def place():
    y = lax.axis_index("frame")
    xz = lax.axis_index("head")
    x = lax.div(xz, 8)
    z = lax.rem(xz, 8)
    return y, x, lax.div(z, 2), lax.rem(z, 2), lax.axis_index("rep")


def remote(src, dst, sent, received, there):
    return pltpu.make_async_remote_copy(
        src_ref=src,
        dst_ref=dst,
        send_sem=sent,
        recv_sem=received,
        device_id=there,
        device_id_type=MESH,
    )


def send(src, dst, sent, received, here, there):
    same = (here[0] == there[0]) & (here[1] == there[1])

    @pl.when(same)
    def _():
        pltpu.make_async_copy(src, dst, received).start()

    @pl.when(jnp.logical_not(same))
    def _():
        remote(src, dst, sent, received, there).start()


def greet(there):
    pl.semaphore_signal(
        pltpu.get_barrier_semaphore(), inc=1, device_id=there, device_id_type=MESH
    )


def wait_bytes(ref, sem):
    pltpu.make_async_copy(ref, ref, sem).wait()


def chunk_of(y, x, zh, zl):
    turn = lax.rem(x + 16 - y - zh, 4)
    return lax.rem(2 * zh + jnp.where(zl == 1, turn + 1, 8 - turn), 8)


def gather_kernel(
    capacity,
    lists_ref,
    q_ref,
    k_ref,
    v_ref,
    q_out,
    k_out,
    v_out,
    k_spread,
    v_spread,
    k_other,
    v_other,
    k_stage,
    v_stage,
    k_relay,
    v_relay,
    send_sem,
    recv_sem,
    relay_sem,
    quarter_sem,
):
    y, x, zh, zl, core = place()
    z = 2 * zh + zl
    here = (y, x * 8 + z, core)
    right, left = lax.rem(x + 1, 4), lax.rem(x + 3, 4)

    def at(x2, zl2):
        return (y, x2 * 8 + 2 * zh + zl2, core)

    chunk = chunk_of(y, x, zh, zl)
    same_chunk = chunk == z
    same_query = lax.rem(y, 2) == zl

    xs = [lax.rem(x + dx, 4) * 8 + chunk for dx in range(4)]
    ys = [2 * number + zl for number in range(4)]

    def greet_senders(i, carry):
        y1, xz1 = lax.rem(y + i, 8), x * 8 + lax.rem(z + i, 8)
        for xz in xs:
            greet((y1, xz, core))
        for y2 in ys:
            greet((y2, xz1, core))
        return carry

    lax.fori_loop(1, 8, greet_senders, 0)
    for xz in xs[1:]:
        greet((y, xz, core))

    @pl.when(jnp.logical_not(same_chunk))
    def _():
        greet((y, xs[0], core))

    for y2 in ys:

        @pl.when(y2 != y)
        def _(y2=y2):
            greet((y2, x * 8 + z, core))

    for mate in (at(right, zl), at(left, zl), at(x, 1 - zl)):
        greet(mate)
    pl.semaphore_wait(
        pltpu.get_barrier_semaphore(),
        2 * HEADS + 3 - same_chunk.astype(jnp.int32) - same_query.astype(jnp.int32),
    )

    planes = [lax.rem(y + 3 * e, 8) for e in range(8)]
    own_copy = same_chunk

    def columns(source, head):
        return source.at[:, pl.ds(pl.multiple_of(head * HEAD_DIM, HEAD_DIM), HEAD_DIM)]

    def spread(source, landing, number):
        def step(quarter, carry):
            zhs = [lax.rem(zh + quarter + r, 4) for r in range(4)]
            offs = [lax.rem(z - 2 * zh2 + 11, 8) - 3 for zh2 in zhs]
            lows = [2 * zh2 + (off > 0).astype(jnp.int32) for zh2, off in zip(zhs, offs)]
            turns = [jnp.where(off > 0, off - 1, -off) + zh2 for off, zh2 in zip(offs, zhs)]
            sent, received = send_sem.at[number], quarter_sem.at[4 * number + quarter]
            for e, y2 in enumerate(planes):
                piece = columns(source, y2 * 4 + zhs[e % 4])
                rows = landing.at[8 * quarter + e // 4 * 4 + x]
                there = (y2, lax.rem(turns[e % 4] + y2, 4) * 8 + lows[e % 4], core)
                if e == 0:
                    send(piece, rows, sent, received, here, there)
                else:
                    remote(piece, rows, sent, received, there).start()
            return carry

        lax.fori_loop(0, 4, step, 0)

    def send_queries(first, last):
        rows = q_out.at[lax.div(y, 2), z]
        odd = x * 8 + lax.rem(y, 2)

        def step(quarter, carry):
            zhs = [lax.rem(zh + quarter + r, 4) for r in range(4)]
            for e, y2 in enumerate(planes):
                piece = columns(q_ref, y2 * 4 + zhs[e % 4])
                there = (y2, 2 * zhs[e % 4] + odd, core)
                if e == 0:
                    send(piece, rows, send_sem.at[2], recv_sem.at[2], here, there)
                else:
                    remote(piece, rows, send_sem.at[2], recv_sem.at[2], there).start()
            return carry

        lax.fori_loop(first, last, step, 0)

    def swap(spread_ref, other_ref, number):
        for quarter in range(4):
            part = pl.ds(8 * quarter, 8)
            wait_bytes(spread_ref.at[part], quarter_sem.at[4 * number + quarter])
            remote(
                spread_ref.at[part],
                other_ref.at[part],
                send_sem.at[3 + number],
                recv_sem.at[3 + number],
                at(x, 1 - zl),
            ).start()

    middle = capacity // 2
    halves = (
        (pl.ds(0, middle), right, left),
        (pl.ds(middle, capacity - middle), left, right),
    )
    mates = (right, left, lax.rem(x + 2, 4), x)
    bases = [(2 * x2 + zl) * SLOTS for x2 in mates]

    def to_mates(side, spread_ref, stage, relay, landing, number):
        def pick(p, carry):
            for mate, base in enumerate(bases):
                stage[side, mate, p] = spread_ref[lists_ref[side * 256 + base + p]]
            return carry

        lax.fori_loop(0, capacity, pick, 0)
        rows = landing.at[:, chunk_of(y, x, zh, zl if side == 0 else 1 - zl)]
        sent, landed = send_sem.at[5 + number], recv_sem.at[5 + number]
        for half, (part, by, _) in enumerate(halves):
            remote(
                stage.at[side, 2, part],
                relay.at[side, part],
                sent,
                relay_sem.at[4 * number + 2 * side + half],
                at(by, zl),
            ).start()
        remote(stage.at[side, 0], rows, sent, landed, at(right, zl)).start()
        remote(stage.at[side, 1], rows, sent, landed, at(left, zl)).start()
        pltpu.make_async_copy(stage.at[side, 3], rows, landed).start()

    def pass_on(side, relay, landing, number):
        for half, (part, there, owner) in enumerate(halves):
            wait_bytes(relay.at[side, part], relay_sem.at[4 * number + 2 * side + half])
            rows = landing.at[part, chunk_of(y, owner, zh, zl if side == 0 else 1 - zl)]
            remote(
                relay.at[side, part], rows, send_sem.at[7 + number], recv_sem.at[5 + number], at(there, zl)
            ).start()

    spread(k_ref, k_spread, 0)
    spread(v_ref, v_spread, 1)
    swap(k_spread, k_other, 0)
    to_mates(0, k_spread, k_stage, k_relay, k_out, 0)
    send_queries(0, 2)
    swap(v_spread, v_other, 1)
    to_mates(0, v_spread, v_stage, v_relay, v_out, 1)
    send_queries(2, 4)
    wait_bytes(k_other, recv_sem.at[3])
    to_mates(1, k_other, k_stage, k_relay, k_out, 0)
    pass_on(0, k_relay, k_out, 0)
    wait_bytes(v_other, recv_sem.at[4])
    to_mates(1, v_other, v_stage, v_relay, v_out, 1)
    pass_on(0, v_relay, v_out, 1)
    pass_on(1, k_relay, k_out, 0)
    pass_on(1, v_relay, v_out, 1)
    wait_bytes(k_spread, send_sem.at[3])
    wait_bytes(v_spread, send_sem.at[4])

    def wait_sent(number, own_copy):
        @pl.when(own_copy)
        def _():
            wait_bytes(k_ref.at[:, pl.ds(0, (HEADS - 1) * HEAD_DIM)], send_sem.at[number])

        @pl.when(jnp.logical_not(own_copy))
        def _():
            wait_bytes(k_spread, send_sem.at[number])

    wait_sent(0, own_copy)
    wait_sent(1, own_copy)
    wait_sent(2, same_query)
    for number, stage, relay in ((0, k_stage, k_relay), (1, v_stage, v_relay)):
        wait_bytes(stage.at[:, pl.ds(0, 3)], send_sem.at[5 + number])
        wait_bytes(relay, send_sem.at[7 + number])
    wait_bytes(q_out, recv_sem.at[2])
    wait_bytes(k_out, recv_sem.at[5])
    wait_bytes(v_out, recv_sem.at[6])


def gather(capacity, lists, queries, key_rows, values):
    any_space = pl.BlockSpec(memory_space=pl.ANY)
    pieces = (GROUP_FRAMES, GROUPS, CHUNK, HEAD_DIM)
    picked = (capacity, GROUPS, CHUNK, HEAD_DIM)
    scratch = [(SLOTS,)] * 4 + [(2, 4, capacity)] * 2 + [(2, capacity)] * 2
    return pl.pallas_call(
        functools.partial(gather_kernel, capacity),
        out_shape=[jax.ShapeDtypeStruct(shape, jnp.bfloat16) for shape in (pieces, picked, picked)],
        in_specs=[pl.BlockSpec(memory_space=pltpu.SMEM), any_space, any_space, any_space],
        out_specs=[any_space] * 3,
        scratch_shapes=[
            *(pltpu.VMEM((*shape, CHUNK, HEAD_DIM), jnp.bfloat16) for shape in scratch),
            pltpu.SemaphoreType.DMA((9,)),
            pltpu.SemaphoreType.DMA((7,)),
            pltpu.SemaphoreType.DMA((8,)),
            pltpu.SemaphoreType.DMA((8,)),
        ],
        compiler_params=pltpu.CompilerParams(
            collective_id=ROOMS.index(capacity), has_side_effects=True, vmem_limit_bytes=40 * 2**20
        ),
    )(lists, queries, key_rows, values)


BLOCK = 128


def attend_kernel(info_ref, q_ref, k_ref, v_ref, o_ref, apart, ones, top, weighted):
    square = (FRAME_PIX, FRAME_PIX)
    apart[...] = jnp.abs(
        lax.broadcasted_iota(jnp.int32, square, 0) - lax.broadcasted_iota(jnp.int32, square, 1)
    )
    ones[...] = jnp.ones_like(ones)

    def tile(own, position, width, first, reach):
        for block in range(FRAME_PIX // BLOCK):
            rows = pl.ds(block * BLOCK, BLOCK)
            low = max(0, block * BLOCK - reach)
            near = pl.ds(low, min(FRAME_PIX, (block + 1) * BLOCK + reach) - low)
            scores = lax.dot_general(
                q_ref[own, rows, :],
                k_ref[position, near, :],
                (((1,), (1,)), ((), ())),
                preferred_element_type=jnp.float32,
            )
            masked = jnp.where(apart[rows, near] < width, scores * SCALE, -1e30)
            high = jnp.max(masked, axis=1, keepdims=True)
            if first:
                new_top = jnp.broadcast_to(high, (BLOCK, HEAD_DIM))
            else:
                old_top = top[rows, :]
                new_top = jnp.maximum(old_top, high)
            weight = jnp.exp2(masked - jnp.concatenate([new_top] * (near.size // HEAD_DIM), axis=1))
            product = jnp.dot(
                weight.astype(jnp.bfloat16),
                jnp.concatenate([v_ref[position, near, :], ones[near, :]], axis=1),
                preferred_element_type=jnp.float32,
            )
            if first:
                weighted[rows, :] = product
            else:
                shrink = jnp.exp2(old_top - new_top)
                weighted[rows, :] = weighted[rows, :] * jnp.concatenate([shrink] * 2, axis=1) + product
            top[rows, :] = new_top

    def one_frame(own, carry):
        code = info_ref[own * SLOTS]
        tile(own, lax.shift_right_logical(code, 10), lax.bitwise_and(code, 1023), True, FRAME_PIX)

        def visit(number, inner):
            code = info_ref[own * SLOTS + number]
            position, width = lax.shift_right_logical(code, 10), lax.bitwise_and(code, 1023)

            @pl.when(width > 256)
            def _():
                tile(own, position, width, False, FRAME_PIX)

            @pl.when((width > 128) & (width <= 256))
            def _():
                tile(own, position, width, False, 256)

            @pl.when(width <= 128)
            def _():
                tile(own, position, width, False, 128)

            return inner

        lax.fori_loop(1, info_ref[GROUP_FRAMES * SLOTS + own], visit, 0)
        o_ref[own] = (weighted[:, :HEAD_DIM] / weighted[:, HEAD_DIM:]).astype(jnp.bfloat16)
        return carry

    lax.fori_loop(0, GROUP_FRAMES, one_frame, 0)


def attend(info, q_local, keys, vals):
    capacity = keys.shape[0]
    vmem = pl.BlockSpec(memory_space=pltpu.VMEM)
    outcome = pl.pallas_call(
        attend_kernel,
        out_shape=jax.ShapeDtypeStruct((GROUP_FRAMES, FRAME_PIX, HEAD_DIM), jnp.bfloat16),
        in_specs=[pl.BlockSpec(memory_space=pltpu.SMEM), vmem, vmem, vmem],
        out_specs=vmem,
        scratch_shapes=[
            pltpu.VMEM((FRAME_PIX, FRAME_PIX), jnp.int32),
            pltpu.VMEM((FRAME_PIX, HEAD_DIM), jnp.bfloat16),
            pltpu.VMEM((FRAME_PIX, HEAD_DIM), jnp.float32),
            pltpu.VMEM((FRAME_PIX, 2 * HEAD_DIM), jnp.float32),
        ],
        compiler_params=pltpu.CompilerParams(vmem_limit_bytes=40 * 2**20),
    )(
        info,
        q_local.reshape(GROUP_FRAMES, FRAME_PIX, HEAD_DIM),
        keys.reshape(capacity, FRAME_PIX, HEAD_DIM),
        vals.reshape(capacity, FRAME_PIX, HEAD_DIM),
    )
    return outcome.reshape(GROUP_FRAMES, GROUPS, CHUNK, HEAD_DIM)


def return_kernel(o_ref, out_ref, send_sem, recv_sem):
    y, x, zh, zl, core = place()
    z = 2 * zh + zl
    here = (y, x * 8 + z, core)
    head = y * 4 + zh
    same = lax.rem(y, 2) == zl

    zs = [x * 8 + 2 * number + lax.rem(y, 2) for number in range(4)]

    def greet_senders(i, carry):
        y1 = lax.rem(y + i, 8)
        for xz in zs:
            greet((y1, xz, core))
        return carry

    lax.fori_loop(1, 8, greet_senders, 0)
    for xz in zs:

        @pl.when(xz != x * 8 + z)
        def _(xz=xz):
            greet((y, xz, core))

    pl.semaphore_wait(pltpu.get_barrier_semaphore(), HEADS - same.astype(jnp.int32))
    places = [lax.rem(z + 3 * e, 8) for e in range(8)]
    rows = out_ref.at[head]

    def step(quarter, carry):
        numbers = [lax.rem(lax.div(y, 2) + quarter + r, 4) for r in range(4)]
        for e, z2 in enumerate(places):
            number = numbers[e % 4]
            piece, there = o_ref.at[number, z2], (2 * number + zl, x * 8 + z2, core)
            if e == 0:
                send(piece, rows, send_sem, recv_sem, here, there)
            else:
                remote(piece, rows, send_sem, recv_sem, there).start()
        return carry

    lax.fori_loop(0, 4, step, 0)
    sent = out_ref.at[pl.ds(0, HEADS - 1)]

    @pl.when(same)
    def _():
        wait_bytes(sent, send_sem)

    @pl.when(jnp.logical_not(same))
    def _():
        wait_bytes(out_ref, send_sem)

    wait_bytes(out_ref, recv_sem)


def send_back(outcome):
    any_space = pl.BlockSpec(memory_space=pl.ANY)
    by_head = pl.pallas_call(
        return_kernel,
        out_shape=jax.ShapeDtypeStruct((HEADS, CHUNK, HEAD_DIM), jnp.bfloat16),
        in_specs=[any_space],
        out_specs=any_space,
        scratch_shapes=[pltpu.SemaphoreType.DMA, pltpu.SemaphoreType.DMA],
        compiler_params=pltpu.CompilerParams(collective_id=len(ROOMS), has_side_effects=True),
    )(outcome)
    return by_head.transpose(1, 0, 2).reshape(CHUNK, HEADS * HEAD_DIM)


def plan_kernel(slot_ref, tiles_ref, lists_ref, info_ref, index_ref):
    y, x, zh, zl, core = place()
    half, single = jnp.bfloat16, jnp.float32

    def flags(condition):
        return jnp.where(condition, 1.0, 0.0)

    def times(left, right):
        return jnp.dot(left.astype(half), right.astype(half), preferred_element_type=single)

    def across(left, right):
        return lax.dot_general(
            left.astype(half), right.astype(half), (((1,), (1,)), ((), ())), preferred_element_type=single
        )

    def iota(rows, columns, dimension):
        return lax.broadcasted_iota(jnp.int32, (rows, columns), dimension)

    diagonal = iota(SLOTS, SLOTS, 0) == iota(SLOTS, SLOTS, 1)
    slots = jnp.sum(jnp.where(diagonal, slot_ref[...], 0), axis=1, keepdims=True)
    on_query = tiles_ref[0:1, :] == slots
    on_key = flags(tiles_ref[1:2, :] == slots)
    widths = tiles_ref[2:3, :]
    coarse = across(jnp.where(on_query, lax.shift_right_logical(widths, 4).astype(single), 0.0), on_key)
    fine = across(jnp.where(on_query, lax.bitwise_and(widths, 15).astype(single), 0.0), on_key)
    slot = iota(GROUPS, SLOTS, 1)
    group = 2 * lax.bitwise_and(slot, 3) + lax.bitwise_and(lax.shift_right_logical(slot, 2), 1)
    in_group = flags(group == iota(GROUPS, SLOTS, 0))
    needed = flags(times(in_group, flags(coarse + fine > 0)) > 0)
    before = flags(iota(SLOTS, SLOTS, 0) < iota(SLOTS, SLOTS, 1))
    rank = times(needed, before)
    order = iota(SLOTS, SLOTS, 0).astype(single)
    picks = [
        flags(rank[g : g + 1] == order) * needed[g : g + 1] for g in range(GROUPS)
    ]
    number = iota(1, SLOTS, 1)
    for side, low in ((0, zl), (1, 1 - zl)):
        source = lax.div(chunk_of(y, x, zh, low), 2)
        eighth = lax.bitwise_and(3 * (y + 8 - lax.shift_right_logical(number, 2)), 7)
        quarter = lax.bitwise_and(zh + 12 - source - eighth, 3)
        spot = quarter * 8 + lax.bitwise_and(eighth, 4) + lax.bitwise_and(number, 3)
        found = across(spot.astype(single), jnp.concatenate(picks, axis=0))
        lists_ref[:, side * 256 : side * 256 + 256] = found.astype(jnp.int32)
    most = jnp.max(jnp.sum(needed, axis=1, keepdims=True), axis=0, keepdims=True)
    index = sum(flags(most > room) for room in ROOMS[:-1])
    index_ref[...] = jnp.broadcast_to(index, (1, 128)).astype(jnp.int32)
    query = iota(GROUP_FRAMES, SLOTS, 0)
    own = flags(iota(GROUP_FRAMES, SLOTS, 1) == GROUP_FRAMES * (2 * query + zl) + x)
    my_coarse, my_fine = times(own, coarse), times(own, fine)
    others = flags(my_coarse + my_fine > 0) * (1.0 - own)
    turn = (1.0 + times(others, before)) * (1.0 - own)
    at = [
        flags(turn[q : q + 1] == order) * (own + others)[q : q + 1] for q in range(GROUP_FRAMES)
    ]
    ones = jnp.ones((1, SLOTS), single)
    my_rank = times(flags(iota(1, GROUPS, 1) == 2 * x + zl), rank)
    place_of = across(my_rank, jnp.concatenate(at, axis=0))
    coarse_of = across(
        ones, jnp.concatenate([at[q] * my_coarse[q : q + 1] for q in range(GROUP_FRAMES)], axis=0)
    )
    fine_of = across(
        ones, jnp.concatenate([at[q] * my_fine[q : q + 1] for q in range(GROUP_FRAMES)], axis=0)
    )
    info_ref[:, :128] = (place_of * 1024 + coarse_of * 16 + fine_of).astype(jnp.int32)
    padded = jnp.concatenate([others, jnp.zeros((128 - GROUP_FRAMES, SLOTS), single)], axis=0)
    info_ref[:, 128:] = 1 + across(ones, padded).astype(jnp.int32)


def plan(slot_frame, radial_tiles):
    vmem = pl.BlockSpec(memory_space=pltpu.VMEM)
    lists, info, index = pl.pallas_call(
        plan_kernel,
        out_shape=[jax.ShapeDtypeStruct((1, size), jnp.int32) for size in (512, 256, 128)],
        in_specs=[vmem] * 2,
        out_specs=[vmem] * 3,
    )(slot_frame.reshape(1, SLOTS), radial_tiles.T)
    return lists.reshape(-1), info.reshape(-1), index[0, 0]


def on_device(queries, key_rows, values, slot_frame, radial_tiles):
    lists, info, index = plan(slot_frame, radial_tiles)

    def run(capacity):
        def branch(lists, info, queries, key_rows, values):
            q_local, keys, vals = gather(capacity, lists, queries, key_rows, values)
            return attend(info, q_local, keys, vals)

        return branch

    outcome = lax.switch(
        index, [run(room) for room in ROOMS], lists, info, queries, key_rows, values
    )
    return send_back(outcome)


def solution(mesh):
    placed = (
        P(("rep", "frame", "head"), None),
        P(("rep", "frame", "head"), None),
        P(("rep", "frame", "head"), None),
        P(),
        P(),
    )
    return jax.shard_map(
        on_device,
        mesh=mesh,
        in_specs=placed,
        out_specs=P(("rep", "frame", "head"), None),
        check_vma=False,
    )
```

```python
import functools
import math

import jax
import jax.numpy as jnp
from jax import lax
from jax.experimental import pallas as pl
from jax.experimental.pallas import tpu as pltpu
from jax.sharding import PartitionSpec as P

HEADS = 32
HEAD_DIM = 128
FRAME_PIX = 512
GROUPS = 8
GROUP_FRAMES = 4
CHUNK = 64
SLOTS = 32
ROOMS = (12, 13, 14, 16, 32)
MESH = pl.DeviceIdType.MESH
SCALE = math.log2(math.e) / math.sqrt(HEAD_DIM)


def place():
    y = lax.axis_index("frame")
    xz = lax.axis_index("head")
    x = lax.div(xz, 8)
    z = lax.rem(xz, 8)
    return y, x, lax.div(z, 2), lax.rem(z, 2), lax.axis_index("rep")


def remote(src, dst, sent, received, there):
    return pltpu.make_async_remote_copy(
        src_ref=src,
        dst_ref=dst,
        send_sem=sent,
        recv_sem=received,
        device_id=there,
        device_id_type=MESH,
    )


def send(src, dst, sent, received, here, there):
    same = (here[0] == there[0]) & (here[1] == there[1])

    @pl.when(same)
    def _():
        pltpu.make_async_copy(src, dst, received).start()

    @pl.when(jnp.logical_not(same))
    def _():
        remote(src, dst, sent, received, there).start()


def greet(there):
    pl.semaphore_signal(
        pltpu.get_barrier_semaphore(), inc=1, device_id=there, device_id_type=MESH
    )


def wait_bytes(ref, sem):
    pltpu.make_async_copy(ref, ref, sem).wait()


def chunk_of(y, x, zh, zl):
    turn = lax.rem(x + 16 - y - zh, 4)
    return lax.rem(2 * zh + jnp.where(zl == 1, turn + 1, 8 - turn), 8)


def gather_kernel(
    capacity,
    lists_ref,
    q_ref,
    k_ref,
    v_ref,
    q_out,
    k_out,
    v_out,
    k_spread,
    v_spread,
    k_other,
    v_other,
    k_stage,
    v_stage,
    k_relay,
    v_relay,
    send_sem,
    recv_sem,
    relay_sem,
    quarter_sem,
):
    y, x, zh, zl, core = place()
    z = 2 * zh + zl
    here = (y, x * 8 + z, core)
    right, left = lax.rem(x + 1, 4), lax.rem(x + 3, 4)

    def at(x2, zl2):
        return (y, x2 * 8 + 2 * zh + zl2, core)

    chunk = chunk_of(y, x, zh, zl)
    same_chunk = chunk == z
    same_query = lax.rem(y, 2) == zl

    xs = [lax.rem(x + dx, 4) * 8 + chunk for dx in range(4)]
    ys = [2 * number + zl for number in range(4)]

    def greet_senders(i, carry):
        y1, xz1 = lax.rem(y + i, 8), x * 8 + lax.rem(z + i, 8)
        for xz in xs:
            greet((y1, xz, core))
        for y2 in ys:
            greet((y2, xz1, core))
        return carry

    lax.fori_loop(1, 8, greet_senders, 0)
    for xz in xs[1:]:
        greet((y, xz, core))

    @pl.when(jnp.logical_not(same_chunk))
    def _():
        greet((y, xs[0], core))

    for y2 in ys:

        @pl.when(y2 != y)
        def _(y2=y2):
            greet((y2, x * 8 + z, core))

    for mate in (at(right, zl), at(left, zl), at(x, 1 - zl)):
        greet(mate)
    pl.semaphore_wait(
        pltpu.get_barrier_semaphore(),
        2 * HEADS + 3 - same_chunk.astype(jnp.int32) - same_query.astype(jnp.int32),
    )

    planes = [lax.rem(y + 3 * e, 8) for e in range(8)]
    own_copy = same_chunk

    def columns(source, head):
        return source.at[:, pl.ds(pl.multiple_of(head * HEAD_DIM, HEAD_DIM), HEAD_DIM)]

    def spread(source, landing, number):
        def step(quarter, carry):
            zhs = [lax.rem(zh + quarter + r, 4) for r in range(4)]
            offs = [lax.rem(z - 2 * zh2 + 11, 8) - 3 for zh2 in zhs]
            lows = [2 * zh2 + (off > 0).astype(jnp.int32) for zh2, off in zip(zhs, offs)]
            turns = [jnp.where(off > 0, off - 1, -off) + zh2 for off, zh2 in zip(offs, zhs)]
            sent, received = send_sem.at[number], quarter_sem.at[4 * number + quarter]
            for e, y2 in enumerate(planes):
                piece = columns(source, y2 * 4 + zhs[e % 4])
                rows = landing.at[8 * quarter + e // 4 * 4 + x]
                there = (y2, lax.rem(turns[e % 4] + y2, 4) * 8 + lows[e % 4], core)
                if e == 0:
                    send(piece, rows, sent, received, here, there)
                else:
                    remote(piece, rows, sent, received, there).start()
            return carry

        lax.fori_loop(0, 4, step, 0)

    def send_queries(first, last):
        rows = q_out.at[lax.div(y, 2), z]
        odd = x * 8 + lax.rem(y, 2)

        def step(quarter, carry):
            zhs = [lax.rem(zh + quarter + r, 4) for r in range(4)]
            for e, y2 in enumerate(planes):
                piece = columns(q_ref, y2 * 4 + zhs[e % 4])
                there = (y2, 2 * zhs[e % 4] + odd, core)
                if e == 0:
                    send(piece, rows, send_sem.at[2], recv_sem.at[2], here, there)
                else:
                    remote(piece, rows, send_sem.at[2], recv_sem.at[2], there).start()
            return carry

        lax.fori_loop(first, last, step, 0)

    def swap(spread_ref, other_ref, number):
        for quarter in range(4):
            part = pl.ds(8 * quarter, 8)
            wait_bytes(spread_ref.at[part], quarter_sem.at[4 * number + quarter])
            remote(
                spread_ref.at[part],
                other_ref.at[part],
                send_sem.at[3 + number],
                recv_sem.at[3 + number],
                at(x, 1 - zl),
            ).start()

    middle = capacity // 2
    halves = (
        (pl.ds(0, middle), right, left),
        (pl.ds(middle, capacity - middle), left, right),
    )
    mates = (right, left, lax.rem(x + 2, 4), x)
    bases = [(2 * x2 + zl) * SLOTS for x2 in mates]

    def to_mates(side, spread_ref, stage, relay, landing, number):
        def pick(p, carry):
            for mate, base in enumerate(bases):
                stage[side, mate, p] = spread_ref[lists_ref[side * 256 + base + p]]
            return carry

        lax.fori_loop(0, capacity, pick, 0)
        rows = landing.at[:, chunk_of(y, x, zh, zl if side == 0 else 1 - zl)]
        sent, landed = send_sem.at[5 + number], recv_sem.at[5 + number]
        for half, (part, by, _) in enumerate(halves):
            remote(
                stage.at[side, 2, part],
                relay.at[side, part],
                sent,
                relay_sem.at[4 * number + 2 * side + half],
                at(by, zl),
            ).start()
        remote(stage.at[side, 0], rows, sent, landed, at(right, zl)).start()
        remote(stage.at[side, 1], rows, sent, landed, at(left, zl)).start()
        pltpu.make_async_copy(stage.at[side, 3], rows, landed).start()

    def pass_on(side, relay, landing, number):
        for half, (part, there, owner) in enumerate(halves):
            wait_bytes(relay.at[side, part], relay_sem.at[4 * number + 2 * side + half])
            rows = landing.at[part, chunk_of(y, owner, zh, zl if side == 0 else 1 - zl)]
            remote(
                relay.at[side, part], rows, send_sem.at[7 + number], recv_sem.at[5 + number], at(there, zl)
            ).start()

    spread(k_ref, k_spread, 0)
    spread(v_ref, v_spread, 1)
    swap(k_spread, k_other, 0)
    to_mates(0, k_spread, k_stage, k_relay, k_out, 0)
    send_queries(0, 1)
    swap(v_spread, v_other, 1)
    to_mates(0, v_spread, v_stage, v_relay, v_out, 1)
    send_queries(1, 4)
    wait_bytes(k_other, recv_sem.at[3])
    to_mates(1, k_other, k_stage, k_relay, k_out, 0)
    pass_on(0, k_relay, k_out, 0)
    wait_bytes(v_other, recv_sem.at[4])
    to_mates(1, v_other, v_stage, v_relay, v_out, 1)
    pass_on(0, v_relay, v_out, 1)
    pass_on(1, k_relay, k_out, 0)
    pass_on(1, v_relay, v_out, 1)
    wait_bytes(k_spread, send_sem.at[3])
    wait_bytes(v_spread, send_sem.at[4])

    def wait_sent(number, own_copy):
        @pl.when(own_copy)
        def _():
            wait_bytes(k_ref.at[:, pl.ds(0, (HEADS - 1) * HEAD_DIM)], send_sem.at[number])

        @pl.when(jnp.logical_not(own_copy))
        def _():
            wait_bytes(k_spread, send_sem.at[number])

    wait_sent(0, own_copy)
    wait_sent(1, own_copy)
    wait_sent(2, same_query)
    for number, stage, relay in ((0, k_stage, k_relay), (1, v_stage, v_relay)):
        wait_bytes(stage.at[:, pl.ds(0, 3)], send_sem.at[5 + number])
        wait_bytes(relay, send_sem.at[7 + number])
    wait_bytes(q_out, recv_sem.at[2])
    wait_bytes(k_out, recv_sem.at[5])
    wait_bytes(v_out, recv_sem.at[6])


def gather(capacity, lists, queries, key_rows, values):
    any_space = pl.BlockSpec(memory_space=pl.ANY)
    pieces = (GROUP_FRAMES, GROUPS, CHUNK, HEAD_DIM)
    picked = (capacity, GROUPS, CHUNK, HEAD_DIM)
    scratch = [(SLOTS,)] * 4 + [(2, 4, capacity)] * 2 + [(2, capacity)] * 2
    return pl.pallas_call(
        functools.partial(gather_kernel, capacity),
        out_shape=[jax.ShapeDtypeStruct(shape, jnp.bfloat16) for shape in (pieces, picked, picked)],
        in_specs=[pl.BlockSpec(memory_space=pltpu.SMEM), any_space, any_space, any_space],
        out_specs=[any_space] * 3,
        scratch_shapes=[
            *(pltpu.VMEM((*shape, CHUNK, HEAD_DIM), jnp.bfloat16) for shape in scratch),
            pltpu.SemaphoreType.DMA((9,)),
            pltpu.SemaphoreType.DMA((7,)),
            pltpu.SemaphoreType.DMA((8,)),
            pltpu.SemaphoreType.DMA((8,)),
        ],
        compiler_params=pltpu.CompilerParams(
            collective_id=ROOMS.index(capacity), has_side_effects=True, vmem_limit_bytes=40 * 2**20
        ),
    )(lists, queries, key_rows, values)


BLOCK = 128


def attend_kernel(info_ref, q_ref, k_ref, v_ref, o_ref, apart, ones, top, weighted):
    square = (FRAME_PIX, FRAME_PIX)
    apart[...] = jnp.abs(
        lax.broadcasted_iota(jnp.int32, square, 0) - lax.broadcasted_iota(jnp.int32, square, 1)
    )
    ones[...] = jnp.ones_like(ones)

    def tile(own, position, width, first, reach):
        size = 2 * BLOCK if reach == FRAME_PIX else BLOCK
        for block in range(FRAME_PIX // size):
            rows = pl.ds(block * size, size)
            low = max(0, block * size - reach)
            near = pl.ds(low, min(FRAME_PIX, (block + 1) * size + reach) - low)
            scores = lax.dot_general(
                q_ref[own, rows, :],
                k_ref[position, near, :],
                (((1,), (1,)), ((), ())),
                preferred_element_type=jnp.float32,
            )
            masked = jnp.where(apart[rows, near] < width, scores * SCALE, -1e30)
            high = jnp.max(masked, axis=1, keepdims=True)
            if first:
                new_top = jnp.broadcast_to(high, (size, HEAD_DIM))
            else:
                old_top = top[rows, :]
                new_top = jnp.maximum(old_top, high)
            weight = jnp.exp2(masked - jnp.concatenate([new_top] * (near.size // HEAD_DIM), axis=1))
            product = jnp.dot(
                weight.astype(jnp.bfloat16),
                jnp.concatenate([v_ref[position, near, :], ones[near, :]], axis=1),
                preferred_element_type=jnp.float32,
            )
            if first:
                weighted[rows, :] = product
            else:
                shrink = jnp.exp2(old_top - new_top)
                weighted[rows, :] = weighted[rows, :] * jnp.concatenate([shrink] * 2, axis=1) + product
            top[rows, :] = new_top

    def one_frame(own, carry):
        code = info_ref[own * SLOTS]
        tile(own, lax.shift_right_logical(code, 10), lax.bitwise_and(code, 1023), True, FRAME_PIX)

        def visit(number, inner):
            code = info_ref[own * SLOTS + number]
            position, width = lax.shift_right_logical(code, 10), lax.bitwise_and(code, 1023)

            @pl.when(width > 256)
            def _():
                tile(own, position, width, False, FRAME_PIX)

            @pl.when((width > 128) & (width <= 256))
            def _():
                tile(own, position, width, False, 256)

            @pl.when(width <= 128)
            def _():
                tile(own, position, width, False, 128)

            return inner

        lax.fori_loop(1, info_ref[GROUP_FRAMES * SLOTS + own], visit, 0)
        o_ref[own] = (weighted[:, :HEAD_DIM] / weighted[:, HEAD_DIM:]).astype(jnp.bfloat16)
        return carry

    lax.fori_loop(0, GROUP_FRAMES, one_frame, 0)


def attend(info, q_local, keys, vals):
    capacity = keys.shape[0]
    vmem = pl.BlockSpec(memory_space=pltpu.VMEM)
    outcome = pl.pallas_call(
        attend_kernel,
        out_shape=jax.ShapeDtypeStruct((GROUP_FRAMES, FRAME_PIX, HEAD_DIM), jnp.bfloat16),
        in_specs=[pl.BlockSpec(memory_space=pltpu.SMEM), vmem, vmem, vmem],
        out_specs=vmem,
        scratch_shapes=[
            pltpu.VMEM((FRAME_PIX, FRAME_PIX), jnp.int32),
            pltpu.VMEM((FRAME_PIX, HEAD_DIM), jnp.bfloat16),
            pltpu.VMEM((FRAME_PIX, HEAD_DIM), jnp.float32),
            pltpu.VMEM((FRAME_PIX, 2 * HEAD_DIM), jnp.float32),
        ],
        compiler_params=pltpu.CompilerParams(vmem_limit_bytes=40 * 2**20),
    )(
        info,
        q_local.reshape(GROUP_FRAMES, FRAME_PIX, HEAD_DIM),
        keys.reshape(capacity, FRAME_PIX, HEAD_DIM),
        vals.reshape(capacity, FRAME_PIX, HEAD_DIM),
    )
    return outcome.reshape(GROUP_FRAMES, GROUPS, CHUNK, HEAD_DIM)


def return_kernel(o_ref, out_ref, send_sem, recv_sem):
    y, x, zh, zl, core = place()
    z = 2 * zh + zl
    here = (y, x * 8 + z, core)
    head = y * 4 + zh
    same = lax.rem(y, 2) == zl

    zs = [x * 8 + 2 * number + lax.rem(y, 2) for number in range(4)]

    def greet_senders(i, carry):
        y1 = lax.rem(y + i, 8)
        for xz in zs:
            greet((y1, xz, core))
        return carry

    lax.fori_loop(1, 8, greet_senders, 0)
    for xz in zs:

        @pl.when(xz != x * 8 + z)
        def _(xz=xz):
            greet((y, xz, core))

    pl.semaphore_wait(pltpu.get_barrier_semaphore(), HEADS - same.astype(jnp.int32))
    places = [lax.rem(z + 3 * e, 8) for e in range(8)]
    rows = out_ref.at[head]

    def step(quarter, carry):
        numbers = [lax.rem(lax.div(y, 2) + quarter + r, 4) for r in range(4)]
        for e, z2 in enumerate(places):
            number = numbers[e % 4]
            piece, there = o_ref.at[number, z2], (2 * number + zl, x * 8 + z2, core)
            if e == 0:
                send(piece, rows, send_sem, recv_sem, here, there)
            else:
                remote(piece, rows, send_sem, recv_sem, there).start()
        return carry

    lax.fori_loop(0, 4, step, 0)
    sent = out_ref.at[pl.ds(0, HEADS - 1)]

    @pl.when(same)
    def _():
        wait_bytes(sent, send_sem)

    @pl.when(jnp.logical_not(same))
    def _():
        wait_bytes(out_ref, send_sem)

    wait_bytes(out_ref, recv_sem)


def send_back(outcome):
    any_space = pl.BlockSpec(memory_space=pl.ANY)
    by_head = pl.pallas_call(
        return_kernel,
        out_shape=jax.ShapeDtypeStruct((HEADS, CHUNK, HEAD_DIM), jnp.bfloat16),
        in_specs=[any_space],
        out_specs=any_space,
        scratch_shapes=[pltpu.SemaphoreType.DMA, pltpu.SemaphoreType.DMA],
        compiler_params=pltpu.CompilerParams(collective_id=len(ROOMS), has_side_effects=True),
    )(outcome)
    return by_head.transpose(1, 0, 2).reshape(CHUNK, HEADS * HEAD_DIM)


def plan_kernel(slot_ref, tiles_ref, lists_ref, info_ref, index_ref):
    y, x, zh, zl, core = place()
    half, single = jnp.bfloat16, jnp.float32

    def flags(condition):
        return jnp.where(condition, 1.0, 0.0)

    def times(left, right):
        return jnp.dot(left.astype(half), right.astype(half), preferred_element_type=single)

    def across(left, right):
        return lax.dot_general(
            left.astype(half), right.astype(half), (((1,), (1,)), ((), ())), preferred_element_type=single
        )

    def iota(rows, columns, dimension):
        return lax.broadcasted_iota(jnp.int32, (rows, columns), dimension)

    diagonal = iota(SLOTS, SLOTS, 0) == iota(SLOTS, SLOTS, 1)
    slots = jnp.sum(jnp.where(diagonal, slot_ref[...], 0), axis=1, keepdims=True)
    on_query = tiles_ref[0:1, :] == slots
    on_key = flags(tiles_ref[1:2, :] == slots)
    widths = tiles_ref[2:3, :]
    coarse = across(jnp.where(on_query, lax.shift_right_logical(widths, 4).astype(single), 0.0), on_key)
    fine = across(jnp.where(on_query, lax.bitwise_and(widths, 15).astype(single), 0.0), on_key)
    slot = iota(GROUPS, SLOTS, 1)
    group = 2 * lax.bitwise_and(slot, 3) + lax.bitwise_and(lax.shift_right_logical(slot, 2), 1)
    in_group = flags(group == iota(GROUPS, SLOTS, 0))
    needed = flags(times(in_group, flags(coarse + fine > 0)) > 0)
    before = flags(iota(SLOTS, SLOTS, 0) < iota(SLOTS, SLOTS, 1))
    rank = times(needed, before)
    order = iota(SLOTS, SLOTS, 0).astype(single)
    picks = [
        flags(rank[g : g + 1] == order) * needed[g : g + 1] for g in range(GROUPS)
    ]
    number = iota(1, SLOTS, 1)
    for side, low in ((0, zl), (1, 1 - zl)):
        source = lax.div(chunk_of(y, x, zh, low), 2)
        eighth = lax.bitwise_and(3 * (y + 8 - lax.shift_right_logical(number, 2)), 7)
        quarter = lax.bitwise_and(zh + 12 - source - eighth, 3)
        spot = quarter * 8 + lax.bitwise_and(eighth, 4) + lax.bitwise_and(number, 3)
        found = across(spot.astype(single), jnp.concatenate(picks, axis=0))
        lists_ref[:, side * 256 : side * 256 + 256] = found.astype(jnp.int32)
    most = jnp.max(jnp.sum(needed, axis=1, keepdims=True), axis=0, keepdims=True)
    index = sum(flags(most > room) for room in ROOMS[:-1])
    index_ref[...] = jnp.broadcast_to(index, (1, 128)).astype(jnp.int32)
    query = iota(GROUP_FRAMES, SLOTS, 0)
    own = flags(iota(GROUP_FRAMES, SLOTS, 1) == GROUP_FRAMES * (2 * query + zl) + x)
    my_coarse, my_fine = times(own, coarse), times(own, fine)
    others = flags(my_coarse + my_fine > 0) * (1.0 - own)
    turn = (1.0 + times(others, before)) * (1.0 - own)
    at = [
        flags(turn[q : q + 1] == order) * (own + others)[q : q + 1] for q in range(GROUP_FRAMES)
    ]
    ones = jnp.ones((1, SLOTS), single)
    my_rank = times(flags(iota(1, GROUPS, 1) == 2 * x + zl), rank)
    place_of = across(my_rank, jnp.concatenate(at, axis=0))
    coarse_of = across(
        ones, jnp.concatenate([at[q] * my_coarse[q : q + 1] for q in range(GROUP_FRAMES)], axis=0)
    )
    fine_of = across(
        ones, jnp.concatenate([at[q] * my_fine[q : q + 1] for q in range(GROUP_FRAMES)], axis=0)
    )
    info_ref[:, :128] = (place_of * 1024 + coarse_of * 16 + fine_of).astype(jnp.int32)
    padded = jnp.concatenate([others, jnp.zeros((128 - GROUP_FRAMES, SLOTS), single)], axis=0)
    info_ref[:, 128:] = 1 + across(ones, padded).astype(jnp.int32)


def plan(slot_frame, radial_tiles):
    vmem = pl.BlockSpec(memory_space=pltpu.VMEM)
    lists, info, index = pl.pallas_call(
        plan_kernel,
        out_shape=[jax.ShapeDtypeStruct((1, size), jnp.int32) for size in (512, 256, 128)],
        in_specs=[vmem] * 2,
        out_specs=[vmem] * 3,
    )(slot_frame.reshape(1, SLOTS), radial_tiles.T)
    return lists.reshape(-1), info.reshape(-1), index[0, 0]


def on_device(queries, key_rows, values, slot_frame, radial_tiles):
    lists, info, index = plan(slot_frame, radial_tiles)

    def run(capacity):
        def branch(lists, info, queries, key_rows, values):
            q_local, keys, vals = gather(capacity, lists, queries, key_rows, values)
            return attend(info, q_local, keys, vals)

        return branch

    outcome = lax.switch(
        index, [run(room) for room in ROOMS], lists, info, queries, key_rows, values
    )
    return send_back(outcome)


def solution(mesh):
    placed = (
        P(("rep", "frame", "head"), None),
        P(("rep", "frame", "head"), None),
        P(("rep", "frame", "head"), None),
        P(),
        P(),
    )
    return jax.shard_map(
        on_device,
        mesh=mesh,
        in_specs=placed,
        out_specs=P(("rep", "frame", "head"), None),
        check_vma=False,
    )
```

```python
import functools
import math

import jax
import jax.numpy as jnp
from jax import lax
from jax.experimental import pallas as pl
from jax.experimental.pallas import tpu as pltpu
from jax.sharding import PartitionSpec as P

HEADS = 32
HEAD_DIM = 128
FRAME_PIX = 512
GROUPS = 8
GROUP_FRAMES = 4
CHUNK = 64
SLOTS = 32
ROOMS = (12, 13, 14, 16, 32)
MESH = pl.DeviceIdType.MESH
SCALE = math.log2(math.e) / math.sqrt(HEAD_DIM)


def place():
    y = lax.axis_index("frame")
    xz = lax.axis_index("head")
    x = lax.div(xz, 8)
    z = lax.rem(xz, 8)
    return y, x, lax.div(z, 2), lax.rem(z, 2), lax.axis_index("rep")


def remote(src, dst, sent, received, there):
    return pltpu.make_async_remote_copy(
        src_ref=src,
        dst_ref=dst,
        send_sem=sent,
        recv_sem=received,
        device_id=there,
        device_id_type=MESH,
    )


def send(src, dst, sent, received, here, there):
    same = (here[0] == there[0]) & (here[1] == there[1])

    @pl.when(same)
    def _():
        pltpu.make_async_copy(src, dst, received).start()

    @pl.when(jnp.logical_not(same))
    def _():
        remote(src, dst, sent, received, there).start()


def greet(there):
    pl.semaphore_signal(
        pltpu.get_barrier_semaphore(), inc=1, device_id=there, device_id_type=MESH
    )


def wait_bytes(ref, sem):
    pltpu.make_async_copy(ref, ref, sem).wait()


def chunk_of(y, x, zh, zl):
    turn = lax.rem(x + 16 - y - zh, 4)
    return lax.rem(2 * zh + jnp.where(zl == 1, turn + 1, 8 - turn), 8)


def gather_kernel(
    capacity,
    lists_ref,
    q_ref,
    k_ref,
    v_ref,
    q_out,
    k_out,
    v_out,
    k_spread,
    v_spread,
    k_other,
    v_other,
    k_stage,
    v_stage,
    k_relay,
    v_relay,
    send_sem,
    recv_sem,
    relay_sem,
    quarter_sem,
):
    y, x, zh, zl, core = place()
    z = 2 * zh + zl
    here = (y, x * 8 + z, core)
    right, left = lax.rem(x + 1, 4), lax.rem(x + 3, 4)

    def at(x2, zl2):
        return (y, x2 * 8 + 2 * zh + zl2, core)

    chunk = chunk_of(y, x, zh, zl)
    same_chunk = chunk == z
    same_query = lax.rem(y, 2) == zl

    xs = [lax.rem(x + dx, 4) * 8 + chunk for dx in range(4)]
    ys = [2 * number + zl for number in range(4)]

    def greet_senders(i, carry):
        y1, xz1 = lax.rem(y + i, 8), x * 8 + lax.rem(z + i, 8)
        for xz in xs:
            greet((y1, xz, core))
        for y2 in ys:
            greet((y2, xz1, core))
        return carry

    lax.fori_loop(1, 8, greet_senders, 0)
    for xz in xs[1:]:
        greet((y, xz, core))

    @pl.when(jnp.logical_not(same_chunk))
    def _():
        greet((y, xs[0], core))

    for y2 in ys:

        @pl.when(y2 != y)
        def _(y2=y2):
            greet((y2, x * 8 + z, core))

    for mate in (at(right, zl), at(left, zl), at(x, 1 - zl)):
        greet(mate)
    pl.semaphore_wait(
        pltpu.get_barrier_semaphore(),
        2 * HEADS + 3 - same_chunk.astype(jnp.int32) - same_query.astype(jnp.int32),
    )

    planes = [lax.rem(y + 3 * e, 8) for e in range(8)]
    own_copy = same_chunk

    def columns(source, head):
        return source.at[:, pl.ds(pl.multiple_of(head * HEAD_DIM, HEAD_DIM), HEAD_DIM)]

    def spread(source, landing, number):
        def step(quarter, carry):
            zhs = [lax.rem(zh + quarter + r, 4) for r in range(4)]
            offs = [lax.rem(z - 2 * zh2 + 11, 8) - 3 for zh2 in zhs]
            lows = [2 * zh2 + (off > 0).astype(jnp.int32) for zh2, off in zip(zhs, offs)]
            turns = [jnp.where(off > 0, off - 1, -off) + zh2 for off, zh2 in zip(offs, zhs)]
            sent, received = send_sem.at[number], quarter_sem.at[4 * number + quarter]
            for e, y2 in enumerate(planes):
                piece = columns(source, y2 * 4 + zhs[e % 4])
                rows = landing.at[8 * quarter + e // 4 * 4 + x]
                there = (y2, lax.rem(turns[e % 4] + y2, 4) * 8 + lows[e % 4], core)
                if e == 0:
                    send(piece, rows, sent, received, here, there)
                else:
                    remote(piece, rows, sent, received, there).start()
            return carry

        lax.fori_loop(0, 4, step, 0)

    def send_queries(first, last):
        rows = q_out.at[lax.div(y, 2), z]
        odd = x * 8 + lax.rem(y, 2)

        def step(quarter, carry):
            zhs = [lax.rem(zh + quarter + r, 4) for r in range(4)]
            for e, y2 in enumerate(planes):
                piece = columns(q_ref, y2 * 4 + zhs[e % 4])
                there = (y2, 2 * zhs[e % 4] + odd, core)
                if e == 0:
                    send(piece, rows, send_sem.at[2], recv_sem.at[2], here, there)
                else:
                    remote(piece, rows, send_sem.at[2], recv_sem.at[2], there).start()
            return carry

        lax.fori_loop(first, last, step, 0)

    def swap(spread_ref, other_ref, number):
        for quarter in range(4):
            part = pl.ds(8 * quarter, 8)
            wait_bytes(spread_ref.at[part], quarter_sem.at[4 * number + quarter])
            remote(
                spread_ref.at[part],
                other_ref.at[part],
                send_sem.at[3 + number],
                recv_sem.at[3 + number],
                at(x, 1 - zl),
            ).start()

    middle = capacity // 2
    halves = (
        (pl.ds(0, middle), right, left),
        (pl.ds(middle, capacity - middle), left, right),
    )
    mates = (right, left, lax.rem(x + 2, 4), x)
    bases = [(2 * x2 + zl) * SLOTS for x2 in mates]

    def to_mates(side, spread_ref, stage, relay, landing, number):
        def pick(p, carry):
            for mate, base in enumerate(bases):
                stage[side, mate, p] = spread_ref[lists_ref[side * 256 + base + p]]
            return carry

        lax.fori_loop(0, capacity, pick, 0)
        rows = landing.at[:, chunk_of(y, x, zh, zl if side == 0 else 1 - zl)]
        sent, landed = send_sem.at[5 + number], recv_sem.at[5 + number]
        for half, (part, by, _) in enumerate(halves):
            remote(
                stage.at[side, 2, part],
                relay.at[side, part],
                sent,
                relay_sem.at[4 * number + 2 * side + half],
                at(by, zl),
            ).start()
        remote(stage.at[side, 0], rows, sent, landed, at(right, zl)).start()
        remote(stage.at[side, 1], rows, sent, landed, at(left, zl)).start()
        pltpu.make_async_copy(stage.at[side, 3], rows, landed).start()

    def pass_on(side, relay, landing, number):
        for half, (part, there, owner) in enumerate(halves):
            wait_bytes(relay.at[side, part], relay_sem.at[4 * number + 2 * side + half])
            rows = landing.at[part, chunk_of(y, owner, zh, zl if side == 0 else 1 - zl)]
            remote(
                relay.at[side, part], rows, send_sem.at[7 + number], recv_sem.at[5 + number], at(there, zl)
            ).start()

    spread(k_ref, k_spread, 0)
    spread(v_ref, v_spread, 1)
    swap(k_spread, k_other, 0)
    to_mates(0, k_spread, k_stage, k_relay, k_out, 0)
    send_queries(0, 1)
    swap(v_spread, v_other, 1)
    to_mates(0, v_spread, v_stage, v_relay, v_out, 1)
    wait_bytes(k_other, recv_sem.at[3])
    to_mates(1, k_other, k_stage, k_relay, k_out, 0)
    send_queries(1, 4)
    pass_on(0, k_relay, k_out, 0)
    wait_bytes(v_other, recv_sem.at[4])
    to_mates(1, v_other, v_stage, v_relay, v_out, 1)
    pass_on(0, v_relay, v_out, 1)
    pass_on(1, k_relay, k_out, 0)
    pass_on(1, v_relay, v_out, 1)
    wait_bytes(k_spread, send_sem.at[3])
    wait_bytes(v_spread, send_sem.at[4])

    def wait_sent(number, own_copy):
        @pl.when(own_copy)
        def _():
            wait_bytes(k_ref.at[:, pl.ds(0, (HEADS - 1) * HEAD_DIM)], send_sem.at[number])

        @pl.when(jnp.logical_not(own_copy))
        def _():
            wait_bytes(k_spread, send_sem.at[number])

    wait_sent(0, own_copy)
    wait_sent(1, own_copy)
    wait_sent(2, same_query)
    for number, stage, relay in ((0, k_stage, k_relay), (1, v_stage, v_relay)):
        wait_bytes(stage.at[:, pl.ds(0, 3)], send_sem.at[5 + number])
        wait_bytes(relay, send_sem.at[7 + number])
    wait_bytes(q_out, recv_sem.at[2])
    wait_bytes(k_out, recv_sem.at[5])
    wait_bytes(v_out, recv_sem.at[6])


def gather(capacity, lists, queries, key_rows, values):
    any_space = pl.BlockSpec(memory_space=pl.ANY)
    pieces = (GROUP_FRAMES, GROUPS, CHUNK, HEAD_DIM)
    picked = (capacity, GROUPS, CHUNK, HEAD_DIM)
    scratch = [(SLOTS,)] * 4 + [(2, 4, capacity)] * 2 + [(2, capacity)] * 2
    return pl.pallas_call(
        functools.partial(gather_kernel, capacity),
        out_shape=[jax.ShapeDtypeStruct(shape, jnp.bfloat16) for shape in (pieces, picked, picked)],
        in_specs=[pl.BlockSpec(memory_space=pltpu.SMEM), any_space, any_space, any_space],
        out_specs=[any_space] * 3,
        scratch_shapes=[
            *(pltpu.VMEM((*shape, CHUNK, HEAD_DIM), jnp.bfloat16) for shape in scratch),
            pltpu.SemaphoreType.DMA((9,)),
            pltpu.SemaphoreType.DMA((7,)),
            pltpu.SemaphoreType.DMA((8,)),
            pltpu.SemaphoreType.DMA((8,)),
        ],
        compiler_params=pltpu.CompilerParams(
            collective_id=ROOMS.index(capacity), has_side_effects=True, vmem_limit_bytes=40 * 2**20
        ),
    )(lists, queries, key_rows, values)


BLOCK = 128


def attend_kernel(info_ref, q_ref, k_ref, v_ref, o_ref, apart, ones, top, weighted):
    square = (FRAME_PIX, FRAME_PIX)
    apart[...] = jnp.abs(
        lax.broadcasted_iota(jnp.int32, square, 0) - lax.broadcasted_iota(jnp.int32, square, 1)
    )
    ones[...] = jnp.ones_like(ones)

    def tile(own, position, width, first, reach):
        size = 2 * BLOCK if reach == FRAME_PIX else BLOCK
        for block in range(FRAME_PIX // size):
            rows = pl.ds(block * size, size)
            low = max(0, block * size - reach)
            near = pl.ds(low, min(FRAME_PIX, (block + 1) * size + reach) - low)
            scores = lax.dot_general(
                q_ref[own, rows, :],
                k_ref[position, near, :],
                (((1,), (1,)), ((), ())),
                preferred_element_type=jnp.float32,
            )
            masked = jnp.where(apart[rows, near] < width, scores * SCALE, -1e30)
            high = jnp.max(masked, axis=1, keepdims=True)
            if first:
                new_top = jnp.broadcast_to(high, (size, HEAD_DIM))
            else:
                old_top = top[rows, :]
                new_top = jnp.maximum(old_top, high)
            weight = jnp.exp2(masked - jnp.concatenate([new_top] * (near.size // HEAD_DIM), axis=1))
            product = jnp.dot(
                weight.astype(jnp.bfloat16),
                jnp.concatenate([v_ref[position, near, :], ones[near, :]], axis=1),
                preferred_element_type=jnp.float32,
            )
            if first:
                weighted[rows, :] = product
            else:
                shrink = jnp.exp2(old_top - new_top)
                weighted[rows, :] = weighted[rows, :] * jnp.concatenate([shrink] * 2, axis=1) + product
            top[rows, :] = new_top

    def one_frame(own, carry):
        code = info_ref[own * SLOTS]
        tile(own, lax.shift_right_logical(code, 10), lax.bitwise_and(code, 1023), True, FRAME_PIX)

        def visit(number, inner):
            code = info_ref[own * SLOTS + number]
            position, width = lax.shift_right_logical(code, 10), lax.bitwise_and(code, 1023)

            @pl.when(width > 256)
            def _():
                tile(own, position, width, False, FRAME_PIX)

            @pl.when((width > 128) & (width <= 256))
            def _():
                tile(own, position, width, False, 256)

            @pl.when(width <= 128)
            def _():
                tile(own, position, width, False, 128)

            return inner

        lax.fori_loop(1, info_ref[GROUP_FRAMES * SLOTS + own], visit, 0)
        o_ref[own] = (weighted[:, :HEAD_DIM] / weighted[:, HEAD_DIM:]).astype(jnp.bfloat16)
        return carry

    lax.fori_loop(0, GROUP_FRAMES, one_frame, 0)


def attend(info, q_local, keys, vals):
    capacity = keys.shape[0]
    vmem = pl.BlockSpec(memory_space=pltpu.VMEM)
    outcome = pl.pallas_call(
        attend_kernel,
        out_shape=jax.ShapeDtypeStruct((GROUP_FRAMES, FRAME_PIX, HEAD_DIM), jnp.bfloat16),
        in_specs=[pl.BlockSpec(memory_space=pltpu.SMEM), vmem, vmem, vmem],
        out_specs=vmem,
        scratch_shapes=[
            pltpu.VMEM((FRAME_PIX, FRAME_PIX), jnp.int32),
            pltpu.VMEM((FRAME_PIX, HEAD_DIM), jnp.bfloat16),
            pltpu.VMEM((FRAME_PIX, HEAD_DIM), jnp.float32),
            pltpu.VMEM((FRAME_PIX, 2 * HEAD_DIM), jnp.float32),
        ],
        compiler_params=pltpu.CompilerParams(vmem_limit_bytes=40 * 2**20),
    )(
        info,
        q_local.reshape(GROUP_FRAMES, FRAME_PIX, HEAD_DIM),
        keys.reshape(capacity, FRAME_PIX, HEAD_DIM),
        vals.reshape(capacity, FRAME_PIX, HEAD_DIM),
    )
    return outcome.reshape(GROUP_FRAMES, GROUPS, CHUNK, HEAD_DIM)


def return_kernel(o_ref, out_ref, send_sem, recv_sem):
    y, x, zh, zl, core = place()
    z = 2 * zh + zl
    here = (y, x * 8 + z, core)
    head = y * 4 + zh
    same = lax.rem(y, 2) == zl

    zs = [x * 8 + 2 * number + lax.rem(y, 2) for number in range(4)]

    def greet_senders(i, carry):
        y1 = lax.rem(y + i, 8)
        for xz in zs:
            greet((y1, xz, core))
        return carry

    lax.fori_loop(1, 8, greet_senders, 0)
    for xz in zs:

        @pl.when(xz != x * 8 + z)
        def _(xz=xz):
            greet((y, xz, core))

    pl.semaphore_wait(pltpu.get_barrier_semaphore(), HEADS - same.astype(jnp.int32))
    places = [lax.rem(z + 3 * e, 8) for e in range(8)]
    rows = out_ref.at[head]

    def step(quarter, carry):
        numbers = [lax.rem(lax.div(y, 2) + quarter + r, 4) for r in range(4)]
        for e, z2 in enumerate(places):
            number = numbers[e % 4]
            piece, there = o_ref.at[number, z2], (2 * number + zl, x * 8 + z2, core)
            if e == 0:
                send(piece, rows, send_sem, recv_sem, here, there)
            else:
                remote(piece, rows, send_sem, recv_sem, there).start()
        return carry

    lax.fori_loop(0, 4, step, 0)
    sent = out_ref.at[pl.ds(0, HEADS - 1)]

    @pl.when(same)
    def _():
        wait_bytes(sent, send_sem)

    @pl.when(jnp.logical_not(same))
    def _():
        wait_bytes(out_ref, send_sem)

    wait_bytes(out_ref, recv_sem)


def send_back(outcome):
    any_space = pl.BlockSpec(memory_space=pl.ANY)
    by_head = pl.pallas_call(
        return_kernel,
        out_shape=jax.ShapeDtypeStruct((HEADS, CHUNK, HEAD_DIM), jnp.bfloat16),
        in_specs=[any_space],
        out_specs=any_space,
        scratch_shapes=[pltpu.SemaphoreType.DMA, pltpu.SemaphoreType.DMA],
        compiler_params=pltpu.CompilerParams(collective_id=len(ROOMS), has_side_effects=True),
    )(outcome)
    return by_head.transpose(1, 0, 2).reshape(CHUNK, HEADS * HEAD_DIM)


def plan_kernel(slot_ref, tiles_ref, lists_ref, info_ref, index_ref):
    y, x, zh, zl, core = place()
    half, single = jnp.bfloat16, jnp.float32

    def flags(condition):
        return jnp.where(condition, 1.0, 0.0)

    def times(left, right):
        return jnp.dot(left.astype(half), right.astype(half), preferred_element_type=single)

    def across(left, right):
        return lax.dot_general(
            left.astype(half), right.astype(half), (((1,), (1,)), ((), ())), preferred_element_type=single
        )

    def iota(rows, columns, dimension):
        return lax.broadcasted_iota(jnp.int32, (rows, columns), dimension)

    diagonal = iota(SLOTS, SLOTS, 0) == iota(SLOTS, SLOTS, 1)
    slots = jnp.sum(jnp.where(diagonal, slot_ref[...], 0), axis=1, keepdims=True)
    on_query = tiles_ref[0:1, :] == slots
    on_key = flags(tiles_ref[1:2, :] == slots)
    widths = tiles_ref[2:3, :]
    coarse = across(jnp.where(on_query, lax.shift_right_logical(widths, 4).astype(single), 0.0), on_key)
    fine = across(jnp.where(on_query, lax.bitwise_and(widths, 15).astype(single), 0.0), on_key)
    slot = iota(GROUPS, SLOTS, 1)
    group = 2 * lax.bitwise_and(slot, 3) + lax.bitwise_and(lax.shift_right_logical(slot, 2), 1)
    in_group = flags(group == iota(GROUPS, SLOTS, 0))
    needed = flags(times(in_group, flags(coarse + fine > 0)) > 0)
    before = flags(iota(SLOTS, SLOTS, 0) < iota(SLOTS, SLOTS, 1))
    rank = times(needed, before)
    order = iota(SLOTS, SLOTS, 0).astype(single)
    picks = [
        flags(rank[g : g + 1] == order) * needed[g : g + 1] for g in range(GROUPS)
    ]
    number = iota(1, SLOTS, 1)
    for side, low in ((0, zl), (1, 1 - zl)):
        source = lax.div(chunk_of(y, x, zh, low), 2)
        eighth = lax.bitwise_and(3 * (y + 8 - lax.shift_right_logical(number, 2)), 7)
        quarter = lax.bitwise_and(zh + 12 - source - eighth, 3)
        spot = quarter * 8 + lax.bitwise_and(eighth, 4) + lax.bitwise_and(number, 3)
        found = across(spot.astype(single), jnp.concatenate(picks, axis=0))
        lists_ref[:, side * 256 : side * 256 + 256] = found.astype(jnp.int32)
    most = jnp.max(jnp.sum(needed, axis=1, keepdims=True), axis=0, keepdims=True)
    index = sum(flags(most > room) for room in ROOMS[:-1])
    index_ref[...] = jnp.broadcast_to(index, (1, 128)).astype(jnp.int32)
    query = iota(GROUP_FRAMES, SLOTS, 0)
    own = flags(iota(GROUP_FRAMES, SLOTS, 1) == GROUP_FRAMES * (2 * query + zl) + x)
    my_coarse, my_fine = times(own, coarse), times(own, fine)
    others = flags(my_coarse + my_fine > 0) * (1.0 - own)
    turn = (1.0 + times(others, before)) * (1.0 - own)
    at = [
        flags(turn[q : q + 1] == order) * (own + others)[q : q + 1] for q in range(GROUP_FRAMES)
    ]
    ones = jnp.ones((1, SLOTS), single)
    my_rank = times(flags(iota(1, GROUPS, 1) == 2 * x + zl), rank)
    place_of = across(my_rank, jnp.concatenate(at, axis=0))
    coarse_of = across(
        ones, jnp.concatenate([at[q] * my_coarse[q : q + 1] for q in range(GROUP_FRAMES)], axis=0)
    )
    fine_of = across(
        ones, jnp.concatenate([at[q] * my_fine[q : q + 1] for q in range(GROUP_FRAMES)], axis=0)
    )
    info_ref[:, :128] = (place_of * 1024 + coarse_of * 16 + fine_of).astype(jnp.int32)
    padded = jnp.concatenate([others, jnp.zeros((128 - GROUP_FRAMES, SLOTS), single)], axis=0)
    info_ref[:, 128:] = 1 + across(ones, padded).astype(jnp.int32)


def plan(slot_frame, radial_tiles):
    vmem = pl.BlockSpec(memory_space=pltpu.VMEM)
    lists, info, index = pl.pallas_call(
        plan_kernel,
        out_shape=[jax.ShapeDtypeStruct((1, size), jnp.int32) for size in (512, 256, 128)],
        in_specs=[vmem] * 2,
        out_specs=[vmem] * 3,
    )(slot_frame.reshape(1, SLOTS), radial_tiles.T)
    return lists.reshape(-1), info.reshape(-1), index[0, 0]


def on_device(queries, key_rows, values, slot_frame, radial_tiles):
    lists, info, index = plan(slot_frame, radial_tiles)

    def run(capacity):
        def branch(lists, info, queries, key_rows, values):
            q_local, keys, vals = gather(capacity, lists, queries, key_rows, values)
            return attend(info, q_local, keys, vals)

        return branch

    outcome = lax.switch(
        index, [run(room) for room in ROOMS], lists, info, queries, key_rows, values
    )
    return send_back(outcome)


def solution(mesh):
    placed = (
        P(("rep", "frame", "head"), None),
        P(("rep", "frame", "head"), None),
        P(("rep", "frame", "head"), None),
        P(),
        P(),
    )
    return jax.shard_map(
        on_device,
        mesh=mesh,
        in_specs=placed,
        out_specs=P(("rep", "frame", "head"), None),
        check_vma=False,
    )
```
